32 devices in a mesh: depth: 1, eta: 32 (over z, y, x, core).
Axes of the slice: x: 2, y: 2, z: 4, core: 2. Of those that a mesh axis runs over, the one named last changes fastest.
Arguments:
- field_in: bfloat16 [2, 128, 32, 2048], P('depth', 'eta'), may hold values from -6 to 6
- grad_out: bfloat16 [2, 128, 32, 2048], P('depth', 'eta'), may hold values from -6 to 6
- spectral_weight: bfloat16 [2, 64, 64, 1024], P(None, 'eta'), may hold values from -0.75 to 0.75
- mlp_in: bfloat16 [32, 64], replicated, may hold values from -1 to 1
- mlp_bias: float32 [64], replicated, may hold values from -3 to 3
- mlp_out: bfloat16 [64, 32], replicated, may hold values from -0.75 to 0.75
Outputs:
- grad_in: float32 [2, 128, 32, 2048], P('depth', 'eta')
- grad_spectral: float32 [2, 64, 64, 1024], P(None, 'eta', 'depth')
- grad_mlp_in: float32 [32, 64], replicated
- grad_mlp_out: float32 [64, 32], replicated
- grad_mlp_bias: float32 [64], replicated
The draws below stay inside these ranges and needn't reach their ends.
All inputs are finite; a program needn't handle non-finite values.
Results may differ from the reference program's by a relative error of at most 0.0087.
Values may be sent and summed in bfloat16 or wider, within the bound.
No kernel may reach another device: no remote copies, remote signals or barrier semaphores. Data moves between devices by JAX's collectives and lax.ppermute only.
A program may use at most 128 MiB of HBM per device.

```python
import math
import jax
import jax.numpy as jnp
from jax import lax

CH = 32
HID = 64
NP = 2048
MP = 64
ME = 64
NE = 128
DEPTH = 2


def block_scale(stream_key, extent, split, smallest, top_value):
    factor_of, own = 1.0, jax.random.fold_in(stream_key, 6)
    for axis_at, blocks in split:
        heights = jnp.exp(jax.random.uniform(jax.random.fold_in(own, axis_at), (blocks,), jnp.float32, smallest / len(split), top_value / len(split)))
        factor_of = factor_of * jnp.repeat(heights, extent[axis_at] // blocks).reshape([-1 if axis == axis_at else 1 for axis in range(len(extent))])
    return factor_of


def normal_values(own_key, extent, width, reach, shards=(), kind=jnp.bfloat16):
    loudness = block_scale(own_key, extent, shards, -0.22, 0.18) if shards else 1.0
    result = jax.random.normal(own_key, extent, jnp.float32) * width * loudness
    return jnp.minimum(jnp.maximum(result, -reach), reach).astype(kind)


def setup_inputs(seed: int = 0) -> dict:
    keys = jax.random.split(jax.random.key(seed), 7)
    field_in = normal_values(keys[0], (DEPTH, NE, CH, NP), 1.0, 6.0, ((1, 32),))
    grad_out = normal_values(keys[1], (DEPTH, NE, CH, NP), 1.0, 6.0, ((1, 32),))
    spectral_weight = normal_values(keys[2], (2, MP, ME, CH * CH), (2 * CH) ** -0.5, 0.75, ((1, 32),))
    mlp_in = normal_values(keys[3], (CH, HID), CH ** -0.5, 1.0)
    mlp_bias = normal_values(keys[4], (HID,), 0.5, 3.0, (), jnp.float32)
    mlp_out = normal_values(keys[5], (HID, CH), HID ** -0.5, 0.75)
    return {"field_in": field_in, "grad_out": grad_out, "spectral_weight": spectral_weight, "mlp_in": mlp_in, "mlp_bias": mlp_bias, "mlp_out": mlp_out}


def phi_tables(n_phi, n_modes):
    cells = jnp.arange(n_phi, dtype=jnp.int32)
    index = jnp.arange(n_modes, dtype=jnp.int32)
    freq = jnp.where(index < n_modes // 2, index, n_phi - n_modes + index)
    theta = 2.0 * math.pi / n_phi * (cells[:, None] * freq[None, :] % n_phi).astype(jnp.float32)
    pairs = jnp.stack([jnp.cos(theta), -jnp.sin(theta)], axis=-1).reshape(n_phi, 2 * n_modes)
    forward = (pairs / math.sqrt(n_phi)).astype(jnp.bfloat16)
    inverse = (pairs.T / math.sqrt(n_modes)).astype(jnp.bfloat16)
    return (forward, inverse)

def eta_tables(n_eta, n_modes, start, count):
    cells = start + jnp.arange(count, dtype=jnp.int32)
    index = jnp.arange(n_modes, dtype=jnp.int32)
    phase = 2.0 * math.pi / n_eta * (cells[:, None] * index[None, :] % n_eta).astype(jnp.float32)
    cosine = jnp.cos(phase)
    sine = jnp.sin(phase)
    return ((cosine / math.sqrt(n_eta)).astype(jnp.bfloat16), (sine / math.sqrt(n_eta)).astype(jnp.bfloat16), cosine.T / math.sqrt(n_modes), sine.T / math.sqrt(n_modes))

def gelu_slope(value):
    normal_cdf = 0.5 * (1.0 + lax.erf(value / math.sqrt(2.0)))
    return normal_cdf + value * jnp.exp(-0.5 * value * value) / math.sqrt(2.0 * math.pi)

def eta_forward(spectra, eta_cos, eta_sin):
    layers, cells, chans, twice = spectra.shape
    parts = spectra.astype(jnp.float32).reshape(layers, cells, chans, twice // 2, 2)
    real_part = parts[..., 0]
    imag_part = parts[..., 1]
    cosf = eta_cos.astype(jnp.float32)
    sinf = eta_sin.astype(jnp.float32)
    hp = lax.Precision.HIGHEST
    zr = jnp.einsum('decj,em->jdmc', real_part, cosf, precision=hp) + jnp.einsum('decj,em->jdmc', imag_part, sinf, precision=hp)
    zi = jnp.einsum('decj,em->jdmc', imag_part, cosf, precision=hp) - jnp.einsum('decj,em->jdmc', real_part, sinf, precision=hp)
    return jnp.stack([zr, zi], axis=2)

def eta_inverse(modes, inv_cos, inv_sin):
    hp = lax.Precision.HIGHEST
    vr = modes[:, :, 0]
    vi = modes[:, :, 1]
    wr = jnp.einsum('jdmc,me->decj', vr, inv_cos, precision=hp) - jnp.einsum('jdmc,me->decj', vi, inv_sin, precision=hp)
    wi = jnp.einsum('jdmc,me->decj', vr, inv_sin, precision=hp) + jnp.einsum('jdmc,me->decj', vi, inv_cos, precision=hp)
    layers, cells, chans, count = wr.shape
    return jnp.stack([wr, wi], axis=-1).reshape(layers, cells, chans, 2 * count).astype(jnp.bfloat16)

def reference(field_in, grad_out, spectral_weight, mlp_in, mlp_bias, mlp_out):
    hp = lax.Precision.HIGHEST
    phi_fwd, phi_inv = phi_tables(NP, MP)
    eta_cos, eta_sin, inv_cos, inv_sin = eta_tables(NE, ME, 0, NE)
    weights = spectral_weight.astype(jnp.float32).reshape(2, MP, ME, CH, CH)
    rr = weights[0]
    ri = weights[1]
    w_in = mlp_in.astype(jnp.float32)
    w_out = mlp_out.astype(jnp.float32)

    def layer(carry, inputs):
        grad_r, grad_i, acc_in, acc_out, acc_bias = carry
        field = inputs[0][None]
        cotan = inputs[1][None]
        xp = jnp.dot(field, phi_fwd, preferred_element_type=jnp.float32).astype(jnp.bfloat16)
        zx = eta_forward(xp, eta_cos, eta_sin)
        zr = zx[:, :, 0]
        zi = zx[:, :, 1]
        vr = jnp.einsum('kdmc,kmco->kdmo', zr, rr, precision=hp) - jnp.einsum('kdmc,kmco->kdmo', zi, ri, precision=hp)
        vi = jnp.einsum('kdmc,kmco->kdmo', zr, ri, precision=hp) + jnp.einsum('kdmc,kmco->kdmo', zi, rr, precision=hp)
        wx = eta_inverse(jnp.stack([vr, vi], axis=2), inv_cos, inv_sin)
        spectral = jnp.dot(wx, phi_inv, preferred_element_type=jnp.float32)
        field32 = field.astype(jnp.float32)
        hidden_pre = jnp.einsum('decp,ch->dehp', field32, w_in) + mlp_bias[None, None, :, None]
        hidden = jax.nn.gelu(hidden_pre, approximate=False).astype(jnp.bfloat16)
        pre = spectral + jnp.einsum('dehp,hc->decp', hidden.astype(jnp.float32), w_out)
        gpre = (cotan.astype(jnp.float32) * gelu_slope(pre)).astype(jnp.bfloat16)
        gp = jnp.dot(gpre, phi_fwd, preferred_element_type=jnp.float32).astype(jnp.bfloat16)
        zg = eta_forward(gp, eta_cos, eta_sin)
        gr = zg[:, :, 0]
        gi = zg[:, :, 1]
        grad_r = grad_r + jnp.einsum('kdmc,kdmo->kmco', zr, gr, precision=hp) + jnp.einsum('kdmc,kdmo->kmco', zi, gi, precision=hp)
        grad_i = grad_i + jnp.einsum('kdmc,kdmo->kmco', zr, gi, precision=hp) - jnp.einsum('kdmc,kdmo->kmco', zi, gr, precision=hp)
        br = jnp.einsum('kdmo,kmco->kdmc', gr, rr, precision=hp) + jnp.einsum('kdmo,kmco->kdmc', gi, ri, precision=hp)
        bi = jnp.einsum('kdmo,kmco->kdmc', gi, rr, precision=hp) - jnp.einsum('kdmo,kmco->kdmc', gr, ri, precision=hp)
        wb = eta_inverse(jnp.stack([br, bi], axis=2), inv_cos, inv_sin)
        back_spec = jnp.dot(wb, phi_inv, preferred_element_type=jnp.float32)
        gpre32 = gpre.astype(jnp.float32)
        hidden_grad = jnp.einsum('decp,hc->dehp', gpre32, w_out) * gelu_slope(hidden_pre)
        hidden_gb = hidden_grad.astype(jnp.bfloat16).astype(jnp.float32)
        grad_field = cotan.astype(jnp.float32) + back_spec + jnp.einsum('dehp,ch->decp', hidden_gb, w_in)
        acc_in = acc_in + jnp.einsum('decp,dehp->ch', field32, hidden_gb)
        acc_out = acc_out + jnp.einsum('dehp,decp->hc', hidden.astype(jnp.float32), gpre32)
        acc_bias = acc_bias + lax.optimization_barrier(jnp.sum(hidden_grad, axis=(0, 1, 3)))
        return ((grad_r, grad_i, acc_in, acc_out, acc_bias), grad_field[0])
    start = (jnp.zeros((MP, ME, CH, CH), jnp.float32), jnp.zeros((MP, ME, CH, CH), jnp.float32), jnp.zeros((CH, HID), jnp.float32), jnp.zeros((HID, CH), jnp.float32), jnp.zeros((HID,), jnp.float32))
    final, grad_in = lax.scan(layer, start, (field_in, grad_out))
    grad_r, grad_i, acc_in, acc_out, acc_bias = final
    factor = math.sqrt(NP * NE / (MP * ME))
    grad_spectral = (jnp.stack([grad_r, grad_i], axis=0) * factor).reshape(2, MP, ME, CH * CH)
    norm = 1.0 / math.sqrt(DEPTH * NE * NP)
    return (grad_in, grad_spectral, acc_in * norm, acc_out * norm, acc_bias * norm)
```

```python
import functools
import math

import jax
import jax.numpy as jnp
import numpy as np
from jax import lax
from jax.experimental import pallas as pl
from jax.experimental.pallas import tpu as pltpu
from jax.sharding import PartitionSpec as P

F32 = jnp.float32
BF16 = jnp.bfloat16
LANES = 128
CHUNK = 256
STEP = 512
LIMIT = 32 * 1024 * 1024


def phi_pairs(n_phi, owned, owners):
    n_modes = owned * owners
    index = np.arange(n_modes)
    freq = np.where(index < n_modes // 2, index, n_phi - n_modes + index)
    theta = 2.0 * np.pi / n_phi * ((np.arange(n_phi)[None, :] * freq[:, None]) % n_phi)
    theta = theta.reshape(owners, owned, n_phi).transpose(1, 0, 2)
    return np.stack([np.cos(theta), -np.sin(theta)]).reshape(2 * n_modes, n_phi)


def eta_tables(cells, owners, n_modes):
    n_eta = cells * owners
    phase = 2.0 * np.pi / n_eta * ((np.arange(n_eta)[None, :] * np.arange(n_modes)[:, None]) % n_eta)
    phase = phase.reshape(n_modes, owners, cells).transpose(0, 2, 1).reshape(n_modes, n_eta)
    cos, sin = np.cos(phase), np.sin(phase)
    forward = np.concatenate([cos, sin]) / math.sqrt(n_eta)
    inverse = np.block([[cos.T, -sin.T], [sin.T, cos.T]]) / math.sqrt(n_modes)
    return forward, inverse


def dot(a, b):
    return jnp.dot(a, b, preferred_element_type=F32)


def dot_rows(a, b):
    return lax.dot_general(a, b, (((1,), (1,)), ((), ())), preferred_element_type=F32)


def split(x):
    high = x.astype(BF16)
    return high, (x - high.astype(F32)).astype(BF16)


def gelu_parts(v):
    square = v * v
    capped = jnp.minimum(square, 27.04)
    poly = -6.666758338545128e-08
    for a in (
        3.1052332348022884e-06, -5.041388393796624e-05, -4.473045135442513e-05,
        0.03634451762350441, 0.7978822527967008,
    ):
        poly = poly * capped + a
    half = 0.5 * jnp.tanh(v * poly)
    density = (1.0 / math.sqrt(2.0 * math.pi)) * jnp.exp2((-0.5 / math.log(2.0)) * square)
    return half, half + v * density


def load(src, dst, sem):
    return pltpu.make_async_copy(src, dst, sem)


def columns(j):
    return pl.ds(pl.multiple_of(j * STEP, STEP), STEP)


def iota(shape, axis):
    return lax.broadcasted_iota(jnp.int32, shape, axis)


def expand_table(chans, width):
    rows, cols = iota((2 * chans, width), 0), iota((2 * chans, width), 1)
    return (rows % chans == cols // chans).astype(F32).astype(BF16)


def spread_table(chans, groups):
    shape = (2 * groups * chans, groups * LANES)
    rows, cols = iota(shape, 0) % (groups * chans), iota(shape, 1)
    same = (rows // chans == cols // LANES) & (rows % chans == cols % chans)
    return same.astype(F32).astype(BF16)


def gather_table(chans, groups):
    shape = (groups * LANES, LANES)
    rows, cols = iota(shape, 0), iota(shape, 1)
    same = (rows // LANES == cols // chans) & (rows % chans == cols % chans)
    return same.astype(F32).astype(BF16)


def collect_table(chans):
    shape = (chans * chans, LANES)
    return (iota(shape, 0) // chans == iota(shape, 1)).astype(F32).astype(BF16)


def pack_spectra(spectra, rows_ref, rows, layers, cells, owners, owned):
    width = spectra.shape[1] // (layers * cells)
    for cell in range(cells):
        for part in range(2):
            pieces = []
            for mode in range(owned):
                top = (part * owned + mode) * owners
                for layer in range(layers):
                    left = (layer * cells + cell) * width
                    pieces.append(spectra[top : top + owners, left : left + width])
            rows_ref[pl.ds(cell * 2 + part, owners, rows), :] = jnp.concatenate(pieces, axis=1)


def xp_kernel(field_h, fwd_h, out, field, fwd, rows_ref, sems, *, sizes):
    layers, cells, owners, owned = sizes
    copies = [load(fwd_h, fwd, sems.at[0]), load(field_h, field, sems.at[1])]
    for copy in copies:
        copy.start()
    for copy in copies:
        copy.wait()
    spectra = dot_rows(fwd[...], field[...])
    pack_spectra(spectra, rows_ref, 8, layers, cells, owners, owned)
    out[...] = rows_ref[...].reshape(out.shape).astype(BF16)


def by_cell(weights, cells):
    rows, cols = weights.shape
    wide = jnp.concatenate([jnp.concatenate([weights] * cells, axis=1)] * cells, axis=0)
    same = iota(wide.shape, 0) // rows == iota(wide.shape, 1) // cols
    return jnp.where(same, wide, 0.0).astype(BF16)


def hidden_kernel(field_h, w_in_h, bias_h, w_out_h, _, *refs, first, count, carried):
    sources, (hidden_h, slope_h, base_h), refs = refs[:carried], refs[carried : carried + 3], refs[carried + 3 :]
    targets, refs = refs[:carried], refs[carried:]
    field, w_in, bias, w_out, wide_bias, pre, hidden, slope, base, ins, outs = refs
    carries = [load(a, b, ins.at[2, n]) for n, (a, b) in enumerate(zip(sources, targets))]
    steps = field.shape[1] // STEP
    chans, hid = w_in.shape
    smalls = ((w_in_h, w_in), (bias_h, bias), (w_out_h, w_out))
    small = [load(a, b, ins.at[1, n]) for n, (a, b) in enumerate(smalls)]
    for copy in small:
        copy.start()
    rows = pl.ds(first * chans, count * chans)
    span = lambda j: pl.ds(j * STEP, STEP)
    read = lambda j: load(field_h.at[rows, span(j)], field.at[:, span(j)], ins.at[0, j])
    pairs = ((hidden, hidden_h), (slope, slope_h), (base, base_h))
    write = lambda n, j: load(
        pairs[n][0].at[:, span(j)], pairs[n][1].at[:, span(j)], outs.at[n, j]
    )
    for j in range(steps):
        read(j).start()
    for copy in carries:
        copy.start()
    for copy in small:
        copy.wait()
    wide = by_cell(w_in[...].astype(F32).T, count)
    back = by_cell(w_out[...].astype(F32), count)
    wide_bias[...] = jnp.broadcast_to(bias[...].T, wide_bias.shape)

    def project(j):
        base[:, span(j)] = dot(back, hidden[:, span(j)])
        write(2, j).start()

    for j in range(steps):
        read(j).wait()
        pre[:, span(j)] = dot(wide, field[:, span(j)])
        if j:
            project(j - 1)
        for left in range(j * STEP, (j + 1) * STEP, CHUNK):
            at = slice(left, left + CHUNK)
            for i in range(count):
                tall = slice(i * hid, (i + 1) * hid)
                v = pre[tall, at] + wide_bias[...]
                half, centred = gelu_parts(v)
                hidden[tall, at] = (v * (0.5 + half)).astype(BF16)
                slope[tall, at] = centred.astype(BF16)
        for n in range(2):
            write(n, j).start()
    project(steps - 1)
    for j in range(steps):
        for n in range(3):
            write(n, j).wait()
    for copy in carries:
        copy.wait()


def unpack(blocks, rows_ref, cells, owners):
    rows = blocks.shape[1]
    rows_ref[...] = blocks[...].astype(F32).reshape(rows_ref.shape)
    part = lambda p: jnp.concatenate(
        [rows_ref[pl.ds(cell * 2 + p, owners, rows), :] for cell in range(cells)], axis=0
    )
    return jnp.concatenate([part(0), part(1)], axis=1).astype(BF16)


def modes_of(spectra, forward):
    both = dot(forward[...], spectra)
    half = both.shape[0] // 2
    real = both[:half, :LANES] + both[half:, LANES:]
    imag = both[:half, LANES:] - both[half:, :LANES]
    return jnp.concatenate([real, imag], axis=0)


def fields_of(modes, inverse, rows_ref, rows, cells, owners):
    high, low = split(modes)
    fields = dot(inverse[...], jnp.concatenate([high, low, high], axis=0))
    for part in range(2):
        for cell in range(cells):
            top = (part * cells + cell) * owners
            rows_ref[pl.ds(cell * 2 + part, owners, rows), :] = fields[top : top + owners]


def widen(modes, pick, chans):
    high, low = split(modes[:, pick * chans : (pick + 1) * chans])
    return jnp.concatenate([high, low], axis=1)


def mix_kernel(
    blocks, weights, forward, inverse, out, modes_h, modes, rows_ref, sems, *, sizes,
):
    layers, cells, owners, owned = sizes
    chans = LANES // (layers * owned)
    expand = expand_table(chans, chans * chans)
    gather = gather_table(chans, layers * owned)
    spectra = unpack(blocks, rows_ref, cells, owners)
    z = modes_of(spectra, forward)
    modes[...] = z
    save = load(modes, modes_h, sems.at[0])
    save.start()
    half = z.shape[0] // 2
    groups = []
    for mode in range(owned):
        wide = jnp.concatenate(
            [widen(z, mode * layers + layer, chans) for layer in range(layers)], axis=0
        )
        sums = [[None, None] for _ in range(layers)]
        for left in range(0, weights.shape[3], CHUNK):
            wr = weights[0, mode, :, left : left + CHUNK].astype(F32)
            wi = weights[1, mode, :, left : left + CHUNK].astype(F32)
            x = dot(wide, expand[:, left : left + CHUNK])
            for layer in range(layers):
                top = 2 * layer * half
                xr, xi = x[top : top + half], x[top + half : top + 2 * half]
                for part, t in enumerate((xr * wr - xi * wi, xr * wi + xi * wr)):
                    t = t[:, :LANES] + t[:, LANES:]
                    old = sums[layer][part]
                    sums[layer][part] = t if old is None else old + t
        groups += [jnp.concatenate(pair, axis=0) for pair in sums]
    high, low = split(jnp.concatenate(groups, axis=1))
    mixed = dot(high, gather) + dot(low, gather)
    fields_of(mixed, inverse, rows_ref, 8, cells, owners)
    out[...] = rows_ref[...].reshape(out.shape).astype(BF16)
    save.wait()


def phi_rows(blocks, rows_ref, layers, cells, owners, owned):
    rows = blocks.shape[1]
    rows_ref[...] = blocks[...].astype(F32).reshape(rows_ref.shape)
    chans = LANES // (layers * owned)
    tall = []
    for part in range(2):
        line = [rows_ref[pl.ds(cell * 2 + part, owners, rows), :] for cell in range(cells)]
        for mode in range(owned):
            pieces = []
            for layer in range(layers):
                left = (mode * layers + layer) * chans
                pieces += [line[cell][:, left : left + chans] for cell in range(cells)]
            tall.append(jnp.concatenate(pieces, axis=1))
    return jnp.concatenate(tall, axis=0).T.astype(BF16)


def gpre_kernel(
    blocks, field_h, cot_h, hidden_a, hidden_b, slope_a, slope_b, base_a, base_b,
    fwd_h, inv_h, w_out_h, out, grad_h,
    field, cot, hidden, slope, base, fwd, inv, w_out, gpre, grad_b, waves, back, pre, grad,
    rows_in, rows_out, slab, ins, outs, *, sizes,
):
    layers, cells, owners, owned = sizes
    n_phi = field.shape[1]
    chans, hid = w_out.shape
    thin, tall = base_a.shape[0], hidden_a.shape[0]
    count = thin // chans
    rows = lambda n: pl.ds(n * thin, thin)
    high = lambda n: pl.ds(n * tall, tall)
    whole = [load(a, b, ins.at[0, n]) for n, (a, b) in enumerate(((w_out_h, w_out), (inv_h, inv), (fwd_h, fwd)))]
    early = [
        [
            load((base_a, base_b)[n], base.at[rows(n), :], ins.at[1 + n, 0]),
            load(cot_h.at[rows(n), :], cot.at[rows(n), :], ins.at[1 + n, 1]),
            load((slope_a, slope_b)[n], slope.at[high(n), :], ins.at[1 + n, 2]),
        ]
        for n in range(2)
    ]
    late = [
        [
            load((hidden_a, hidden_b)[n], hidden.at[high(n), :], ins.at[1 + n, 3]),
            load(field_h.at[rows(n), :], field.at[rows(n), :], ins.at[1 + n, 4]),
        ]
        for n in range(2)
    ]
    writes = [load(grad_b.at[high(n), :], grad_h.at[high(n), :], outs.at[n]) for n in range(2)]
    for copy in (*whole[:2], *early[0], *early[1], whole[2], *late[0], *late[1]):
        copy.start()
    waves[...] = phi_rows(blocks, rows_in, layers, cells, owners, owned)
    whole[0].wait()
    back[...] = by_cell(w_out[...].astype(F32).T, count)
    whole[1].wait()

    def products(n):
        here, up = slice(n * thin, (n + 1) * thin), slice(n * tall, (n + 1) * tall)
        spectra = dot_rows(fwd[...], gpre[here, :])
        part_out = dot_rows(hidden[up, :], gpre[here, :])
        part_in = dot_rows(grad_b[up, :], field[here, :])
        diagonal = lambda x: sum(
            x[i * hid : (i + 1) * hid, i * chans : (i + 1) * chans] for i in range(count)
        )
        return spectra, diagonal(part_in), diagonal(part_out)

    total = jnp.zeros((hid, LANES), F32)
    results = []
    for n in range(2):
        here, up = slice(n * thin, (n + 1) * thin), slice(n * tall, (n + 1) * tall)
        pre[here, :] = dot(waves[here, :], inv[...])
        for copy in early[n]:
            copy.wait()
        if n:
            for copy in (whole[2], *late[0]):
                copy.wait()
            results.append(products(0))
        for left in range(0, n_phi, CHUNK):
            at = slice(left, left + CHUNK)
            for top in range(here.start, here.stop, hid):
                tile = slice(top, top + hid)
                g = 0.5 + gelu_parts(pre[tile, at] + base[tile, at])[1]
                gpre[tile, at] = (cot[tile, at].astype(F32) * g).astype(BF16)
        for left in range(0, n_phi, STEP):
            grad[up, left : left + STEP] = dot(back[...], gpre[here, left : left + STEP])
        for left in range(0, n_phi, CHUNK):
            at = slice(left, left + CHUNK)
            for top in range(up.start, up.stop, hid):
                tile = slice(top, top + hid)
                g = grad[tile, at] * (0.5 + slope[tile, at].astype(F32))
                grad_b[tile, at] = g.astype(BF16)
                total = total + (g[:, :LANES] + g[:, LANES:])
        writes[n].start()
    for copy in late[1]:
        copy.wait()
    results.append(products(1))
    spectra = jnp.concatenate([r[0] for r in results], axis=1)
    pack_spectra(spectra, rows_out, 16, layers, cells, owners, owned)
    part_in, part_out = results[0][1] + results[1][1], results[0][2] + results[1][2]
    bias = jnp.sum(total, axis=1, keepdims=True)
    zeros = jnp.zeros((hid, LANES - 2 * chans), F32)
    full = jnp.concatenate([part_in, part_out, zeros], axis=1)
    full = jnp.where(iota((hid, LANES), 1) == 2 * chans, bias, full)
    high = full.astype(BF16).astype(F32)
    each = hid // owners
    for at, value in enumerate((high, full - high)):
        slab[...] = value
        for row in range(each):
            rows_out[pl.ds(8 + at * each + row, owners, 16), :] = slab[pl.ds(row, owners, each), :]
    for row in range(8 + 2 * each, 16):
        rows_out[pl.ds(row, owners, 16), :] = jnp.zeros((owners, LANES), F32)
    out[...] = rows_out[...].reshape(out.shape).astype(BF16)
    for write in writes:
        write.wait()


def mlp_grad_kernel(cot_h, grad_h, w_in_h, inv_h, out, inv, cot, grad_b, w_in, sems, *, count):
    chans, hid = w_in.shape
    half = cot.shape[0] // 2
    copies = [load(w_in_h, w_in, sems.at[0])]
    for n in range(2):
        low, high = pl.ds(n * half, half), pl.ds(n * half // chans * hid, half // chans * hid)
        copies.append(load(cot_h.at[low, :], cot.at[low, :], sems.at[1 + 2 * n]))
        copies.append(load(grad_h.at[high, :], grad_b.at[high, :], sems.at[2 + 2 * n]))
    copies.append(load(inv_h, inv, sems.at[5]))
    for copy in copies:
        copy.start()
    copies[0].wait()
    weights = by_cell(w_in[...].astype(F32), count)
    for n in range(2):
        for copy in copies[1 + 2 * n : 3 + 2 * n]:
            copy.wait()
        low = slice(n * half, (n + 1) * half)
        high = slice(low.start // chans * hid, low.stop // chans * hid)
        for left in range(0, cot.shape[1], STEP):
            at = slice(left, left + STEP)
            out[low, at] = cot[low, at].astype(F32) + dot(weights, grad_b[high, at])
    copies[5].wait()


def back_kernel(
    blocks, weights, forward, inverse, _, out, modes_h, modes, rows_ref, sems, *, sizes, each,
):
    layers, cells, owners, owned = sizes
    chans = LANES // (layers * owned)
    spread = spread_table(chans, layers * owned)
    collect = collect_table(chans)
    spectra = unpack(blocks, rows_ref, cells, owners)
    z = modes_of(spectra, forward)
    modes[...] = z
    save = load(modes, modes_h, sems.at[0])
    save.start()
    totals = []
    for row in range(each):
        at = 8 + row
        total = jnp.sum(
            rows_ref[pl.ds(at, owners, 16), :] + rows_ref[pl.ds(at + each, owners, 16), :],
            axis=0,
            keepdims=True,
        )
        totals.append(total)
    half = z.shape[0] // 2
    high, low = split(z)
    wide = dot(jnp.concatenate([high, low], axis=1), spread)
    pieces = []
    for mode in range(owned):
        acc = None
        for left in range(0, weights.shape[3], CHUNK):
            wr = weights[0, mode, :, left : left + CHUNK].astype(F32)
            wi = weights[1, mode, :, left : left + CHUNK].astype(F32)
            terms = []
            for layer in range(layers):
                pick = (mode * layers + layer) * LANES
                g = jnp.concatenate([wide[:, pick : pick + LANES]] * (CHUNK // LANES), axis=1)
                gr, gi = g[:half], g[half:]
                terms += [(gr * wr + gi * wi).astype(BF16), (gi * wr - gr * wi).astype(BF16)]
            s = dot(jnp.concatenate(terms, axis=0), collect[left : left + CHUNK, :])
            acc = s if acc is None else acc + s
        acc = [acc[2 * n * half : 2 * (n + 1) * half] for n in range(layers)]
        pieces += [a[:, :chans] for a in acc]
    fields_of(jnp.concatenate(pieces, axis=1), inverse, rows_ref, 16, cells, owners)
    for row, total in enumerate(totals):
        high = total.astype(BF16).astype(F32)
        rows_ref[pl.ds(8 + row, owners, 16), :] = jnp.broadcast_to(high, (owners, LANES))
        rows_ref[pl.ds(8 + each + row, owners, 16), :] = jnp.broadcast_to(total - high, (owners, LANES))
    out[...] = rows_ref[...].reshape(out.shape).astype(BF16)
    save.wait()


def weight_grad_kernel(zx_h, zg_h, out_h, zx, zg, out, sems, *, sizes, factor):
    layers, owned = sizes[0], sizes[3]
    chans = LANES // (layers * owned)
    copies = [load(a, b, sems.at[n]) for n, (a, b) in enumerate(((zx_h, zx), (zg_h, zg)))]
    for copy in copies:
        copy.start()
    expand = expand_table(chans, chans * chans)
    spread = spread_table(chans, layers * owned)
    for copy in copies:
        copy.wait()
    z = zx[...] * factor
    half = z.shape[0] // 2
    high, low = split(zg[...])
    wide = dot(jnp.concatenate([high, low], axis=1), spread)
    saves = []
    for mode in range(owned):
        split_z = [widen(z, mode * layers + layer, chans) for layer in range(layers)]
        for left in range(0, out.shape[3], CHUNK):
            real = imag = 0.0
            for layer in range(layers):
                x = dot(split_z[layer], expand[:, left : left + CHUNK])
                xr, xi = x[:half], x[half:]
                pick = (mode * layers + layer) * LANES
                g = jnp.concatenate([wide[:, pick : pick + LANES]] * (CHUNK // LANES), axis=1)
                gr, gi = g[:half], g[half:]
                real = real + (xr * gr + xi * gi)
                imag = imag + (xr * gi - xi * gr)
            out[0, mode, :, left : left + CHUNK] = real
            out[1, mode, :, left : left + CHUNK] = imag
        for part in range(2):
            saves.append(
                load(out.at[part, mode], out_h.at[part, mode], sems.at[2 + part * owned + mode])
            )
            saves[-1].start()
    for save in saves:
        save.wait()


def final_kernel(
    blocks, base, inv, _, out_h, in_h, out_w_h, bias_h, out, rows_ref, slab, turned, outs, *, sizes, norm,
):
    layers, cells, owners, owned = sizes
    chans = in_h.shape[0]
    count = 4
    span = base.shape[0] // count
    waves = phi_rows(blocks, rows_ref, layers, cells, owners, owned)
    hid = slab.shape[0]
    each = hid // owners
    for row in range(each):
        slab[pl.ds(row, owners, each), :] = (
            rows_ref[pl.ds(8 + row, owners, 16), :] + rows_ref[pl.ds(8 + each + row, owners, 16), :]
        ) * norm
    turned[...] = slab[...].T
    writes = [
        load(turned.at[pl.ds(n * chans, h.shape[0]), :], h, outs.at[1, n])
        for n, h in enumerate((in_h, out_w_h, bias_h))
    ]
    for write in writes:
        write.start()
    for j in range(count):
        here, rows = slice(j * span, (j + 1) * span), pl.ds(j * span, span)
        for left in range(0, base.shape[1], STEP):
            at = slice(left, left + STEP)
            out[here, at] = base[here, at] + dot(waves[here], inv[:, at])
        writes.append(load(out.at[rows, :], out_h.at[rows, :], outs.at[0, j]))
        writes[-1].start()
    for write in writes:
        write.wait()


def call(kernel, ins, outs, scratch, flops, *args, **static):
    space = {"h": pltpu.HBM, "v": pltpu.VMEM, "w": pltpu.VMEM}
    keep = {"h": pltpu.HBM, "w": pltpu.VMEM}
    shapes = [jax.ShapeDtypeStruct(s, d) for _, s, d in outs]
    size = lambda x: math.prod(x.shape) * x.dtype.itemsize
    moved = sum(size(x) for x in (*args, *shapes))
    args = [
        pltpu.with_memory_space_constraint(x, keep[k]) if k in keep else x
        for k, x in zip(ins, args)
    ]
    return pl.pallas_call(
        functools.partial(kernel, **static),
        out_shape=[
            keep[o[0]](x.shape, x.dtype) if o[0] in keep else x for o, x in zip(outs, shapes)
        ],
        in_specs=[pl.BlockSpec(memory_space=space[k]) for k in ins],
        out_specs=[pl.BlockSpec(memory_space=space[k]) for k, _, _ in outs],
        scratch_shapes=[
            pltpu.SemaphoreType.DMA(s) if d is None else pltpu.VMEM(s, d) for s, d in scratch
        ],
        compiler_params=pltpu.CompilerParams(vmem_limit_bytes=LIMIT),
        cost_estimate=pl.CostEstimate(
            flops=flops,
            bytes_accessed=moved,
            transcendentals=0,
        ),
    )(*args)


def local(field_in, grad_out, spectral_weight, mlp_in, mlp_bias, mlp_out):
    layers, cells, chans, n_phi = field_in.shape
    owners = lax.axis_size("eta")
    depth = lax.axis_size("depth")
    n_eta = cells * owners
    owned = spectral_weight.shape[1]
    n_eta_modes = spectral_weight.shape[2]
    n_phi_modes = owned * owners
    hid = mlp_in.shape[1]
    count = layers * cells
    each = hid // owners
    sizes = (layers, cells, owners, owned)
    pairs = phi_pairs(n_phi, owned, owners)
    phi_fwd = jnp.asarray(pairs / math.sqrt(n_phi), BF16)
    phi_inv = jnp.asarray(pairs / math.sqrt(n_phi_modes), BF16)
    forward, inverse = eta_tables(cells, owners, n_eta_modes)
    forward = jnp.asarray(forward, BF16)
    inverse_high = inverse.astype(BF16)
    inverse_low = (inverse - inverse_high.astype(np.float64)).astype(BF16)
    inverse = jnp.asarray(np.concatenate([inverse_high, inverse_high, inverse_low], axis=1))

    thin = (count * chans, n_phi)
    tall = (count * hid, n_phi)
    field = field_in.reshape(thin)
    cot = grad_out.reshape(thin)
    w_out = mlp_out.T
    steps = n_phi // STEP
    exchange = lambda x: lax.all_to_all(x, "eta", 0, 0, tiled=True)
    small = (owners, 8, LANES)
    large = (owners, 16, LANES)
    modes = (2 * n_eta_modes, LANES)
    small_rows = ((owners * 8, LANES), F32)
    large_rows = ((owners * 16, LANES), F32)
    table = ((2 * n_phi_modes, n_phi), BF16)
    grid_mul = 2 * count * n_phi * chans

    (xp,) = call(
        xp_kernel, "hh", [("w", small, BF16)],
        [(thin, BF16), table, small_rows, ((2,), None)],
        grid_mul * 2 * n_phi_modes, field, phi_fwd, sizes=sizes,
    )
    xp = exchange(xp)
    half = count // 2
    part = (half * hid, n_phi)
    half_thin = (half * chans, n_phi)

    def hidden_half(first, after, *carried):
        return call(
            hidden_kernel, "hhhhh" + "h" * len(carried),
            [
                ("h", part, BF16), ("h", part, BF16), ("h", half_thin, F32),
                *(("w", x.shape, x.dtype) for x in carried),
            ],
            [
                (half_thin, BF16), (mlp_in.shape, BF16), ((1, hid), F32), (w_out.shape, BF16),
                ((hid, CHUNK), F32), (part, F32), (part, BF16), (part, BF16), (half_thin, F32),
                ((3, max(steps, 3)), None), ((3, steps), None),
            ],
            grid_mul * hid, field, mlp_in, mlp_bias[None], w_out, after, *carried,
            first=first, count=half, carried=len(carried),
        )

    hidden_a, slope_a, base_a, weights, forward, inverse = hidden_half(
        0, w_out, spectral_weight, forward, inverse
    )
    wx, zx = call(
        mix_kernel, "vwww", [("w", small, BF16), ("h", modes, F32)],
        [(modes, F32), small_rows, ((1,), None)],
        1 << 24, xp, weights, forward, inverse, sizes=sizes,
    )
    wx = exchange(wx)
    hidden_b, slope_b, base_b = hidden_half(half, zx)
    gp, hidden_gb = call(
        gpre_kernel, "vhhhhhhhhhhh", [("w", large, BF16), ("h", tall, BF16)],
        [
            (thin, BF16), (thin, BF16), (tall, BF16), (tall, BF16), (thin, F32), table, table,
            (w_out.shape, BF16), (thin, BF16), (tall, BF16),
            ((count * chans, 2 * n_phi_modes), BF16), ((half * hid, half * chans), BF16),
            (thin, F32), (tall, F32), small_rows, large_rows, ((hid, LANES), F32),
            ((3, 5), None), ((2,), None),
        ],
        grid_mul * (4 * n_phi_modes + 4 * hid), wx, field, cot,
        hidden_a, hidden_b, slope_a, slope_b, base_a, base_b, phi_fwd, phi_inv, w_out, sizes=sizes,
    )
    gp = exchange(gp)
    partial, inverse_phi = call(
        mlp_grad_kernel, "hhhh", [("w", thin, F32), ("w", phi_inv.shape, BF16)],
        [(thin, BF16), (tall, BF16), (mlp_in.shape, BF16), ((6,), None)],
        grid_mul * hid, cot, hidden_gb, mlp_in, phi_inv, count=half,
    )
    wb, zg = call(
        back_kernel, "vwwww", [("w", large, BF16), ("h", modes, F32)],
        [(modes, F32), large_rows, ((1,), None)],
        1 << 24, gp, weights, forward, inverse, partial, sizes=sizes, each=each,
    )
    wb = exchange(wb)
    factor = math.sqrt(n_phi * n_eta / (n_phi_modes * n_eta_modes))
    grad_shape = (2, owned, n_eta_modes, chans * chans)
    (grad_spectral,) = call(
        weight_grad_kernel, "hh", [("h", grad_shape, F32)],
        [(modes, F32), (modes, F32), (grad_shape, F32), ((2 + 2 * owned,), None)],
        1 << 24, zx, zg, sizes=sizes, factor=factor,
    )
    norm = 1.0 / math.sqrt(layers * depth * n_eta * n_phi)
    grad_in, total_in, total_out, total_bias = call(
        final_kernel, "vwwh",
        [("h", thin, F32), ("h", (chans, hid), F32), ("h", (chans, hid), F32), ("h", (1, hid), F32)],
        [
            (thin, F32), large_rows, ((hid, LANES), F32), ((LANES, hid), F32), ((2, 4), None),
        ],
        grid_mul * 2 * n_phi_modes, wb, partial, inverse_phi, grad_spectral, sizes=sizes, norm=norm,
    )
    if depth > 1:
        grad_spectral = lax.psum_scatter(grad_spectral, "depth", scatter_dimension=2, tiled=True)
        total_in, total_out, total_bias = lax.psum((total_in, total_out, total_bias), "depth")
    return (grad_in.reshape(field_in.shape), grad_spectral, total_in, total_out.T, total_bias[0])


def solution(mesh):
    return jax.shard_map(
        local,
        mesh=mesh,
        in_specs=(
            P("depth", "eta", None, None),
            P("depth", "eta", None, None),
            P(None, "eta", None, None),
            P(),
            P(),
            P(),
        ),
        out_specs=(P("depth", "eta", None, None), P(None, "eta", "depth", None), P(), P(), P()),
        check_vma=False,
    )
```

```python
import functools
import math

import jax
import jax.numpy as jnp
import numpy as np
from jax import lax
from jax.experimental import pallas as pl
from jax.experimental.pallas import tpu as pltpu
from jax.sharding import PartitionSpec as P

F32 = jnp.float32
BF16 = jnp.bfloat16
LANES = 128
CHUNK = 256
STEP = 512
LIMIT = 32 * 1024 * 1024


def phi_pairs(n_phi, owned, owners):
    n_modes = owned * owners
    index = np.arange(n_modes)
    freq = np.where(index < n_modes // 2, index, n_phi - n_modes + index)
    theta = 2.0 * np.pi / n_phi * ((np.arange(n_phi)[None, :] * freq[:, None]) % n_phi)
    theta = theta.reshape(owners, owned, n_phi).transpose(1, 0, 2)
    return np.stack([np.cos(theta), -np.sin(theta)]).reshape(2 * n_modes, n_phi)


def eta_tables(cells, owners, n_modes):
    n_eta = cells * owners
    phase = 2.0 * np.pi / n_eta * ((np.arange(n_eta)[None, :] * np.arange(n_modes)[:, None]) % n_eta)
    phase = phase.reshape(n_modes, owners, cells).transpose(0, 2, 1).reshape(n_modes, n_eta)
    cos, sin = np.cos(phase), np.sin(phase)
    forward = np.concatenate([cos, sin]) / math.sqrt(n_eta)
    inverse = np.block([[cos.T, -sin.T], [sin.T, cos.T]]) / math.sqrt(n_modes)
    return forward, inverse


def dot(a, b):
    return jnp.dot(a, b, preferred_element_type=F32)


def dot_rows(a, b):
    return lax.dot_general(a, b, (((1,), (1,)), ((), ())), preferred_element_type=F32)


def split(x):
    high = x.astype(BF16)
    return high, (x - high.astype(F32)).astype(BF16)


def gelu_parts(v):
    square = v * v
    capped = jnp.minimum(square, 27.04)
    poly = -6.666758338545128e-08
    for a in (
        3.1052332348022884e-06, -5.041388393796624e-05, -4.473045135442513e-05,
        0.03634451762350441, 0.7978822527967008,
    ):
        poly = poly * capped + a
    half = 0.5 * jnp.tanh(v * poly)
    density = (1.0 / math.sqrt(2.0 * math.pi)) * jnp.exp2((-0.5 / math.log(2.0)) * square)
    return half, half + v * density


def load(src, dst, sem):
    return pltpu.make_async_copy(src, dst, sem)


def columns(j):
    return pl.ds(pl.multiple_of(j * STEP, STEP), STEP)


def iota(shape, axis):
    return lax.broadcasted_iota(jnp.int32, shape, axis)


def expand_table(chans, width):
    rows, cols = iota((2 * chans, width), 0), iota((2 * chans, width), 1)
    return (rows % chans == cols // chans).astype(F32).astype(BF16)


def spread_table(chans, groups):
    shape = (2 * groups * chans, groups * LANES)
    rows, cols = iota(shape, 0) % (groups * chans), iota(shape, 1)
    same = (rows // chans == cols // LANES) & (rows % chans == cols % chans)
    return same.astype(F32).astype(BF16)


def gather_table(chans, groups):
    shape = (groups * LANES, LANES)
    rows, cols = iota(shape, 0), iota(shape, 1)
    same = (rows // LANES == cols // chans) & (rows % chans == cols % chans)
    return same.astype(F32).astype(BF16)


def collect_table(chans):
    shape = (chans * chans, LANES)
    return (iota(shape, 0) // chans == iota(shape, 1)).astype(F32).astype(BF16)


def pack_spectra(spectra, rows_ref, rows, layers, cells, owners, owned):
    width = spectra.shape[1] // (layers * cells)
    for cell in range(cells):
        for part in range(2):
            pieces = []
            for mode in range(owned):
                top = (part * owned + mode) * owners
                for layer in range(layers):
                    left = (layer * cells + cell) * width
                    pieces.append(spectra[top : top + owners, left : left + width])
            rows_ref[pl.ds(cell * 2 + part, owners, rows), :] = jnp.concatenate(pieces, axis=1)


def xp_kernel(fwd_h, field_h, *refs, sizes):
    layers, cells, owners, owned = sizes
    smalls, out, field, targets, (fwd, rows_ref, sems) = refs[:3], refs[3], refs[4], refs[5:8], refs[8:]
    pairs = ((fwd_h, fwd), (field_h, field), *zip(smalls, targets))
    copies = [load(a, b, sems.at[n]) for n, (a, b) in enumerate(pairs)]
    for copy in copies:
        copy.start()
    for copy in copies:
        copy.wait()
    spectra = dot_rows(fwd[...], field[...])
    pack_spectra(spectra, rows_ref, 8, layers, cells, owners, owned)
    out[...] = rows_ref[...].reshape(out.shape).astype(BF16)


def by_cell(weights, cells):
    rows, cols = weights.shape
    wide = jnp.concatenate([jnp.concatenate([weights] * cells, axis=1)] * cells, axis=0)
    same = iota(wide.shape, 0) // rows == iota(wide.shape, 1) // cols
    return jnp.where(same, wide, 0.0).astype(BF16)


def hidden_kernel(field, w_in, bias, w_out, _, *refs, first, count, carried):
    sources, (hidden_h, slope_h, base_h), refs = refs[:carried], refs[carried : carried + 3], refs[carried + 3 :]
    targets, refs = refs[:carried], refs[carried:]
    wide_bias, pre, hidden, slope, ins, outs, *own = refs
    base = own[0] if own else base_h
    carries = [load(a, b, ins.at[n]) for n, (a, b) in enumerate(zip(sources, targets))]
    for copy in carries:
        copy.start()
    steps = field.shape[1] // STEP
    chans, hid = w_in.shape
    rows = pl.ds(first * chans, count * chans)
    span = lambda j: pl.ds(j * STEP, STEP)
    pairs = ((hidden, hidden_h), (slope, slope_h), (base, base_h))
    write = lambda n, j: load(
        pairs[n][0].at[:, span(j)], pairs[n][1].at[:, span(j)], outs.at[n, j]
    )
    wide = by_cell(w_in[...].astype(F32).T, count)
    back = by_cell(w_out[...].astype(F32), count)
    wide_bias[...] = jnp.broadcast_to(bias[...].T, wide_bias.shape)

    def project(j):
        base[:, span(j)] = dot(back, hidden[:, span(j)])
        if own:
            write(2, j).start()

    for j in range(steps):
        pre[:, span(j)] = dot(wide, field[rows, span(j)])
        if j:
            project(j - 1)
        for left in range(j * STEP, (j + 1) * STEP, CHUNK):
            at = slice(left, left + CHUNK)
            for i in range(count):
                tall = slice(i * hid, (i + 1) * hid)
                v = pre[tall, at] + wide_bias[...]
                half, centred = gelu_parts(v)
                hidden[tall, at] = (v * (0.5 + half)).astype(BF16)
                slope[tall, at] = centred.astype(BF16)
        for n in range(2):
            write(n, j).start()
    project(steps - 1)
    for j in range(steps):
        for n in range(3 if own else 2):
            write(n, j).wait()
    for copy in carries:
        copy.wait()


def unpack(blocks, rows_ref, cells, owners):
    rows = blocks.shape[1]
    rows_ref[...] = blocks[...].astype(F32).reshape(rows_ref.shape)
    part = lambda p: jnp.concatenate(
        [rows_ref[pl.ds(cell * 2 + p, owners, rows), :] for cell in range(cells)], axis=0
    )
    return jnp.concatenate([part(0), part(1)], axis=1).astype(BF16)


def modes_of(spectra, forward):
    both = dot(forward[...], spectra)
    half = both.shape[0] // 2
    real = both[:half, :LANES] + both[half:, LANES:]
    imag = both[:half, LANES:] - both[half:, :LANES]
    return jnp.concatenate([real, imag], axis=0)


def fields_of(modes, inverse, rows_ref, rows, cells, owners):
    high, low = split(modes)
    fields = dot(inverse[...], jnp.concatenate([high, low, high], axis=0))
    for part in range(2):
        for cell in range(cells):
            top = (part * cells + cell) * owners
            rows_ref[pl.ds(cell * 2 + part, owners, rows), :] = fields[top : top + owners]


def widen(modes, pick, chans):
    high, low = split(modes[:, pick * chans : (pick + 1) * chans])
    return jnp.concatenate([high, low], axis=1)


def mix_kernel(
    blocks, weights, forward, inverse, out, modes_h, modes, rows_ref, sems, *, sizes,
):
    layers, cells, owners, owned = sizes
    chans = LANES // (layers * owned)
    expand = expand_table(chans, chans * chans)
    gather = gather_table(chans, layers * owned)
    spectra = unpack(blocks, rows_ref, cells, owners)
    z = modes_of(spectra, forward)
    modes[...] = z
    save = load(modes, modes_h, sems.at[0])
    save.start()
    half = z.shape[0] // 2
    groups = []
    for mode in range(owned):
        wide = jnp.concatenate(
            [widen(z, mode * layers + layer, chans) for layer in range(layers)], axis=0
        )
        sums = [[None, None] for _ in range(layers)]
        for left in range(0, weights.shape[3], CHUNK):
            wr = weights[0, mode, :, left : left + CHUNK].astype(F32)
            wi = weights[1, mode, :, left : left + CHUNK].astype(F32)
            x = dot(wide, expand[:, left : left + CHUNK])
            for layer in range(layers):
                top = 2 * layer * half
                xr, xi = x[top : top + half], x[top + half : top + 2 * half]
                for part, t in enumerate((xr * wr - xi * wi, xr * wi + xi * wr)):
                    t = t[:, :LANES] + t[:, LANES:]
                    old = sums[layer][part]
                    sums[layer][part] = t if old is None else old + t
        groups += [jnp.concatenate(pair, axis=0) for pair in sums]
    high, low = split(jnp.concatenate(groups, axis=1))
    mixed = dot(high, gather) + dot(low, gather)
    fields_of(mixed, inverse, rows_ref, 8, cells, owners)
    out[...] = rows_ref[...].reshape(out.shape).astype(BF16)
    save.wait()


def phi_rows(blocks, rows_ref, layers, cells, owners, owned):
    rows = blocks.shape[1]
    rows_ref[...] = blocks[...].astype(F32).reshape(rows_ref.shape)
    chans = LANES // (layers * owned)
    tall = []
    for part in range(2):
        line = [rows_ref[pl.ds(cell * 2 + part, owners, rows), :] for cell in range(cells)]
        for mode in range(owned):
            pieces = []
            for layer in range(layers):
                left = (mode * layers + layer) * chans
                pieces += [line[cell][:, left : left + chans] for cell in range(cells)]
            tall.append(jnp.concatenate(pieces, axis=1))
    return jnp.concatenate(tall, axis=0).T.astype(BF16)


def gpre_kernel(
    blocks, cot, base_a, inv, w_out, field_h, hidden_a, hidden_b, slope_a, slope_b, base_h,
    fwd_h, out, grad_h,
    field, hidden, slope, base_b, fwd, gpre, grad_b, waves, back, pre, grad,
    rows_in, rows_out, slab, ins, outs, *, sizes,
):
    layers, cells, owners, owned = sizes
    n_phi = field.shape[1]
    chans, hid = w_out.shape
    thin, tall = base_a.shape[0], hidden_a.shape[0]
    count = thin // chans
    rows = lambda n: pl.ds(n * thin, thin)
    high = lambda n: pl.ds(n * tall, tall)
    bases = (base_a, base_b)
    others = [load(fwd_h, fwd, ins.at[2, 0]), load(base_h, base_b, ins.at[2, 1])]
    slopes = [
        load((slope_a, slope_b)[n], slope.at[high(n), :], ins.at[n, 0]) for n in range(2)
    ]
    late = [
        [
            load((hidden_a, hidden_b)[n], hidden.at[high(n), :], ins.at[n, 1]),
            load(field_h.at[rows(n), :], field.at[rows(n), :], ins.at[n, 2]),
        ]
        for n in range(2)
    ]
    writes = [load(grad_b.at[high(n), :], grad_h.at[high(n), :], outs.at[n]) for n in range(2)]
    for copy in (slopes[0], others[1], others[0], *late[0], slopes[1], *late[1]):
        copy.start()
    waves[...] = phi_rows(blocks, rows_in, layers, cells, owners, owned)
    back[...] = by_cell(w_out[...].astype(F32).T, count)

    def products(n):
        here, up = slice(n * thin, (n + 1) * thin), slice(n * tall, (n + 1) * tall)
        spectra = dot_rows(fwd[...], gpre[here, :])
        part_out = dot_rows(hidden[up, :], gpre[here, :])
        part_in = dot_rows(grad_b[up, :], field[here, :])
        diagonal = lambda x: sum(
            x[i * hid : (i + 1) * hid, i * chans : (i + 1) * chans] for i in range(count)
        )
        return spectra, diagonal(part_in), diagonal(part_out)

    total = jnp.zeros((hid, LANES), F32)
    results = []
    for n in range(2):
        here, up = slice(n * thin, (n + 1) * thin), slice(n * tall, (n + 1) * tall)
        pre[here, :] = dot(waves[here, :], inv[...])
        if n:
            for copy in (*others, *late[0], slopes[1]):
                copy.wait()
            results.append(products(0))
        for left in range(0, n_phi, CHUNK):
            at = slice(left, left + CHUNK)
            for top in range(here.start, here.stop, hid):
                tile = slice(top, top + hid)
                base = bases[n][top - here.start : top - here.start + hid, at]
                g = 0.5 + gelu_parts(pre[tile, at] + base)[1]
                gpre[tile, at] = (cot[tile, at].astype(F32) * g).astype(BF16)
        for left in range(0, n_phi, STEP):
            grad[up, left : left + STEP] = dot(back[...], gpre[here, left : left + STEP])
        if n == 0:
            slopes[0].wait()
        for left in range(0, n_phi, CHUNK):
            at = slice(left, left + CHUNK)
            for top in range(up.start, up.stop, hid):
                tile = slice(top, top + hid)
                g = grad[tile, at] * (0.5 + slope[tile, at].astype(F32))
                grad_b[tile, at] = g.astype(BF16)
                total = total + (g[:, :LANES] + g[:, LANES:])
        writes[n].start()
    for copy in late[1]:
        copy.wait()
    results.append(products(1))
    spectra = jnp.concatenate([r[0] for r in results], axis=1)
    pack_spectra(spectra, rows_out, 16, layers, cells, owners, owned)
    part_in, part_out = results[0][1] + results[1][1], results[0][2] + results[1][2]
    bias = jnp.sum(total, axis=1, keepdims=True)
    zeros = jnp.zeros((hid, LANES - 2 * chans), F32)
    full = jnp.concatenate([part_in, part_out, zeros], axis=1)
    full = jnp.where(iota((hid, LANES), 1) == 2 * chans, bias, full)
    high = full.astype(BF16).astype(F32)
    each = hid // owners
    for at, value in enumerate((high, full - high)):
        slab[...] = value
        for row in range(each):
            rows_out[pl.ds(8 + at * each + row, owners, 16), :] = slab[pl.ds(row, owners, each), :]
    for row in range(8 + 2 * each, 16):
        rows_out[pl.ds(row, owners, 16), :] = jnp.zeros((owners, LANES), F32)
    out[...] = rows_out[...].reshape(out.shape).astype(BF16)
    for write in writes:
        write.wait()


def mlp_grad_kernel(cot_h, grad_h, w_in_h, inv_h, out, inv, cot, grad_b, w_in, sems, *, count):
    chans, hid = w_in.shape
    half = cot.shape[0] // 2
    copies = [load(w_in_h, w_in, sems.at[0])]
    for n in range(2):
        low, high = pl.ds(n * half, half), pl.ds(n * half // chans * hid, half // chans * hid)
        copies.append(load(cot_h.at[low, :], cot.at[low, :], sems.at[1 + 2 * n]))
        copies.append(load(grad_h.at[high, :], grad_b.at[high, :], sems.at[2 + 2 * n]))
    copies.append(load(inv_h, inv, sems.at[5]))
    for copy in copies:
        copy.start()
    copies[0].wait()
    weights = by_cell(w_in[...].astype(F32), count)
    for n in range(2):
        for copy in copies[1 + 2 * n : 3 + 2 * n]:
            copy.wait()
        low = slice(n * half, (n + 1) * half)
        high = slice(low.start // chans * hid, low.stop // chans * hid)
        for left in range(0, cot.shape[1], STEP):
            at = slice(left, left + STEP)
            out[low, at] = cot[low, at].astype(F32) + dot(weights, grad_b[high, at])
    copies[5].wait()


def back_kernel(
    blocks, weights, forward, inverse, _, out, modes_h, modes, rows_ref, sems, *, sizes, each,
):
    layers, cells, owners, owned = sizes
    chans = LANES // (layers * owned)
    spread = spread_table(chans, layers * owned)
    collect = collect_table(chans)
    spectra = unpack(blocks, rows_ref, cells, owners)
    z = modes_of(spectra, forward)
    modes[...] = z
    save = load(modes, modes_h, sems.at[0])
    save.start()
    totals = []
    for row in range(each):
        at = 8 + row
        total = jnp.sum(
            rows_ref[pl.ds(at, owners, 16), :] + rows_ref[pl.ds(at + each, owners, 16), :],
            axis=0,
            keepdims=True,
        )
        totals.append(total)
    half = z.shape[0] // 2
    high, low = split(z)
    wide = dot(jnp.concatenate([high, low], axis=1), spread)
    pieces = []
    for mode in range(owned):
        acc = None
        for left in range(0, weights.shape[3], CHUNK):
            wr = weights[0, mode, :, left : left + CHUNK].astype(F32)
            wi = weights[1, mode, :, left : left + CHUNK].astype(F32)
            terms = []
            for layer in range(layers):
                pick = (mode * layers + layer) * LANES
                g = jnp.concatenate([wide[:, pick : pick + LANES]] * (CHUNK // LANES), axis=1)
                gr, gi = g[:half], g[half:]
                terms += [(gr * wr + gi * wi).astype(BF16), (gi * wr - gr * wi).astype(BF16)]
            s = dot(jnp.concatenate(terms, axis=0), collect[left : left + CHUNK, :])
            acc = s if acc is None else acc + s
        acc = [acc[2 * n * half : 2 * (n + 1) * half] for n in range(layers)]
        pieces += [a[:, :chans] for a in acc]
    fields_of(jnp.concatenate(pieces, axis=1), inverse, rows_ref, 16, cells, owners)
    for row, total in enumerate(totals):
        high = total.astype(BF16).astype(F32)
        rows_ref[pl.ds(8 + row, owners, 16), :] = jnp.broadcast_to(high, (owners, LANES))
        rows_ref[pl.ds(8 + each + row, owners, 16), :] = jnp.broadcast_to(total - high, (owners, LANES))
    out[...] = rows_ref[...].reshape(out.shape).astype(BF16)
    save.wait()


def weight_grad_kernel(zx_h, zg_h, out_h, zx, zg, out, sems, *, sizes, factor):
    layers, owned = sizes[0], sizes[3]
    chans = LANES // (layers * owned)
    copies = [load(a, b, sems.at[n]) for n, (a, b) in enumerate(((zx_h, zx), (zg_h, zg)))]
    for copy in copies:
        copy.start()
    expand = expand_table(chans, chans * chans)
    spread = spread_table(chans, layers * owned)
    for copy in copies:
        copy.wait()
    z = zx[...] * factor
    half = z.shape[0] // 2
    high, low = split(zg[...])
    wide = dot(jnp.concatenate([high, low], axis=1), spread)
    saves = []
    for mode in range(owned):
        split_z = [widen(z, mode * layers + layer, chans) for layer in range(layers)]
        for left in range(0, out.shape[3], CHUNK):
            real = imag = 0.0
            for layer in range(layers):
                x = dot(split_z[layer], expand[:, left : left + CHUNK])
                xr, xi = x[:half], x[half:]
                pick = (mode * layers + layer) * LANES
                g = jnp.concatenate([wide[:, pick : pick + LANES]] * (CHUNK // LANES), axis=1)
                gr, gi = g[:half], g[half:]
                real = real + (xr * gr + xi * gi)
                imag = imag + (xr * gi - xi * gr)
            out[0, mode, :, left : left + CHUNK] = real
            out[1, mode, :, left : left + CHUNK] = imag
        for part in range(2):
            saves.append(
                load(out.at[part, mode], out_h.at[part, mode], sems.at[2 + part * owned + mode])
            )
            saves[-1].start()
    for save in saves:
        save.wait()


def final_kernel(
    blocks, base, inv, _, out_h, in_h, out_w_h, bias_h, out, rows_ref, slab, turned, outs, *, sizes, norm,
):
    layers, cells, owners, owned = sizes
    chans = in_h.shape[0]
    count = 4
    span = base.shape[0] // count
    waves = phi_rows(blocks, rows_ref, layers, cells, owners, owned)
    hid = slab.shape[0]
    each = hid // owners
    for row in range(each):
        slab[pl.ds(row, owners, each), :] = (
            rows_ref[pl.ds(8 + row, owners, 16), :] + rows_ref[pl.ds(8 + each + row, owners, 16), :]
        ) * norm
    turned[...] = slab[...].T
    writes = [
        load(turned.at[pl.ds(n * chans, h.shape[0]), :], h, outs.at[1, n])
        for n, h in enumerate((in_h, out_w_h, bias_h))
    ]
    for write in writes:
        write.start()
    for j in range(count):
        here, rows = slice(j * span, (j + 1) * span), pl.ds(j * span, span)
        for left in range(0, base.shape[1], STEP):
            at = slice(left, left + STEP)
            out[here, at] = base[here, at] + dot(waves[here], inv[:, at])
        writes.append(load(out.at[rows, :], out_h.at[rows, :], outs.at[0, j]))
        writes[-1].start()
    for write in writes:
        write.wait()


def call(kernel, ins, outs, scratch, flops, *args, **static):
    space = {"h": pltpu.HBM, "v": pltpu.VMEM, "w": pltpu.VMEM}
    keep = {"h": pltpu.HBM, "w": pltpu.VMEM}
    shapes = [jax.ShapeDtypeStruct(s, d) for _, s, d in outs]
    size = lambda x: math.prod(x.shape) * x.dtype.itemsize
    moved = sum(size(x) for x in (*args, *shapes))
    args = [
        pltpu.with_memory_space_constraint(x, keep[k]) if k in keep else x
        for k, x in zip(ins, args)
    ]
    return pl.pallas_call(
        functools.partial(kernel, **static),
        out_shape=[
            keep[o[0]](x.shape, x.dtype) if o[0] in keep else x for o, x in zip(outs, shapes)
        ],
        in_specs=[pl.BlockSpec(memory_space=space[k]) for k in ins],
        out_specs=[pl.BlockSpec(memory_space=space[k]) for k, _, _ in outs],
        scratch_shapes=[
            pltpu.SemaphoreType.DMA(s) if d is None else pltpu.VMEM(s, d) for s, d in scratch
        ],
        compiler_params=pltpu.CompilerParams(vmem_limit_bytes=LIMIT),
        cost_estimate=pl.CostEstimate(
            flops=flops,
            bytes_accessed=moved,
            transcendentals=0,
        ),
    )(*args)


def local(field_in, grad_out, spectral_weight, mlp_in, mlp_bias, mlp_out):
    layers, cells, chans, n_phi = field_in.shape
    owners = lax.axis_size("eta")
    depth = lax.axis_size("depth")
    n_eta = cells * owners
    owned = spectral_weight.shape[1]
    n_eta_modes = spectral_weight.shape[2]
    n_phi_modes = owned * owners
    hid = mlp_in.shape[1]
    count = layers * cells
    each = hid // owners
    sizes = (layers, cells, owners, owned)
    pairs = phi_pairs(n_phi, owned, owners)
    phi_fwd = jnp.asarray(pairs / math.sqrt(n_phi), BF16)
    phi_inv = jnp.asarray(pairs / math.sqrt(n_phi_modes), BF16)
    forward, inverse = eta_tables(cells, owners, n_eta_modes)
    forward = jnp.asarray(forward, BF16)
    inverse_high = inverse.astype(BF16)
    inverse_low = (inverse - inverse_high.astype(np.float64)).astype(BF16)
    inverse = jnp.asarray(np.concatenate([inverse_high, inverse_high, inverse_low], axis=1))

    thin = (count * chans, n_phi)
    tall = (count * hid, n_phi)
    field = field_in.reshape(thin)
    cot = grad_out.reshape(thin)
    w_out = mlp_out.T
    steps = n_phi // STEP
    exchange = lambda x: lax.all_to_all(x, "eta", 0, 0, tiled=True)
    small = (owners, 8, LANES)
    large = (owners, 16, LANES)
    modes = (2 * n_eta_modes, LANES)
    small_rows = ((owners * 8, LANES), F32)
    large_rows = ((owners * 16, LANES), F32)
    table = ((2 * n_phi_modes, n_phi), BF16)
    grid_mul = 2 * count * n_phi * chans

    smalls = (mlp_in, mlp_bias[None], w_out)
    xp, field_v, w_in_v, bias_v, w_out_v = call(
        xp_kernel, "hhhhh",
        [("v", small, BF16), ("w", thin, BF16), *(("w", x.shape, x.dtype) for x in smalls)],
        [table, small_rows, ((5,), None)],
        grid_mul * 2 * n_phi_modes, phi_fwd, field, *smalls, sizes=sizes,
    )
    xp = exchange(xp)
    half = count // 2
    part = (half * hid, n_phi)
    half_thin = (half * chans, n_phi)

    def hidden_half(first, after, keep_base, *carried):
        return call(
            hidden_kernel, "wwwwh" + "h" * len(carried),
            [
                ("h", part, BF16), ("h", part, BF16), (keep_base, half_thin, F32),
                *(("w", x.shape, x.dtype) for x in carried),
            ],
            [
                ((hid, CHUNK), F32), (part, F32), (part, BF16), (part, BF16),
                ((len(carried),), None), ((3, steps), None),
                *([(half_thin, F32)] if keep_base == "h" else []),
            ],
            grid_mul * hid, field_v, w_in_v, bias_v, w_out_v, after, *carried,
            first=first, count=half, carried=len(carried),
        )

    hidden_a, slope_a, base_a, weights, forward, inverse = hidden_half(
        0, w_out, "w", spectral_weight, forward, inverse
    )
    wx, zx = call(
        mix_kernel, "vwww", [("v", small, BF16), ("h", modes, F32)],
        [(modes, F32), small_rows, ((1,), None)],
        1 << 24, xp, weights, forward, inverse, sizes=sizes,
    )
    wx = exchange(wx)
    hidden_b, slope_b, base_b, cot_v, inv_v = hidden_half(half, zx, "h", cot, phi_inv)
    gp, hidden_gb = call(
        gpre_kernel, "vwwwwhhhhhhh", [("v", large, BF16), ("h", tall, BF16)],
        [
            (thin, BF16), (tall, BF16), (tall, BF16), (half_thin, F32), table,
            (thin, BF16), (tall, BF16),
            ((count * chans, 2 * n_phi_modes), BF16), ((half * hid, half * chans), BF16),
            (thin, F32), (tall, F32), small_rows, large_rows, ((hid, LANES), F32),
            ((3, 3), None), ((2,), None),
        ],
        grid_mul * (4 * n_phi_modes + 4 * hid), wx, cot_v, base_a, inv_v, w_out_v,
        field, hidden_a, hidden_b, slope_a, slope_b, base_b, phi_fwd, sizes=sizes,
    )
    gp = exchange(gp)
    partial, inverse_phi = call(
        mlp_grad_kernel, "hhhh", [("w", thin, F32), ("w", phi_inv.shape, BF16)],
        [(thin, BF16), (tall, BF16), (mlp_in.shape, BF16), ((6,), None)],
        grid_mul * hid, cot, hidden_gb, mlp_in, phi_inv, count=half,
    )
    wb, zg = call(
        back_kernel, "vwwww", [("w", large, BF16), ("h", modes, F32)],
        [(modes, F32), large_rows, ((1,), None)],
        1 << 24, gp, weights, forward, inverse, partial, sizes=sizes, each=each,
    )
    wb = exchange(wb)
    factor = math.sqrt(n_phi * n_eta / (n_phi_modes * n_eta_modes))
    grad_shape = (2, owned, n_eta_modes, chans * chans)
    (grad_spectral,) = call(
        weight_grad_kernel, "hh", [("h", grad_shape, F32)],
        [(modes, F32), (modes, F32), (grad_shape, F32), ((2 + 2 * owned,), None)],
        1 << 24, zx, zg, sizes=sizes, factor=factor,
    )
    norm = 1.0 / math.sqrt(layers * depth * n_eta * n_phi)
    grad_in, total_in, total_out, total_bias = call(
        final_kernel, "vwwh",
        [("h", thin, F32), ("h", (chans, hid), F32), ("h", (chans, hid), F32), ("h", (1, hid), F32)],
        [
            (thin, F32), large_rows, ((hid, LANES), F32), ((LANES, hid), F32), ((2, 4), None),
        ],
        grid_mul * 2 * n_phi_modes, wb, partial, inverse_phi, grad_spectral, sizes=sizes, norm=norm,
    )
    if depth > 1:
        grad_spectral = lax.psum_scatter(grad_spectral, "depth", scatter_dimension=2, tiled=True)
        total_in, total_out, total_bias = lax.psum((total_in, total_out, total_bias), "depth")
    return (grad_in.reshape(field_in.shape), grad_spectral, total_in, total_out.T, total_bias[0])


def solution(mesh):
    return jax.shard_map(
        local,
        mesh=mesh,
        in_specs=(
            P("depth", "eta", None, None),
            P("depth", "eta", None, None),
            P(None, "eta", None, None),
            P(),
            P(),
            P(),
        ),
        out_specs=(P("depth", "eta", None, None), P(None, "eta", "depth", None), P(), P(), P()),
        check_vma=False,
    )
```

```python
import functools
import math

import jax
import jax.numpy as jnp
import numpy as np
from jax import lax
from jax.experimental import pallas as pl
from jax.experimental.pallas import tpu as pltpu
from jax.sharding import PartitionSpec as P

F32 = jnp.float32
BF16 = jnp.bfloat16
LANES = 128
CHUNK = 256
STEP = 512
LIMIT = 32 * 1024 * 1024


def phi_pairs(n_phi, owned, owners):
    n_modes = owned * owners
    index = np.arange(n_modes)
    freq = np.where(index < n_modes // 2, index, n_phi - n_modes + index)
    theta = 2.0 * np.pi / n_phi * ((np.arange(n_phi)[None, :] * freq[:, None]) % n_phi)
    theta = theta.reshape(owners, owned, n_phi).transpose(1, 0, 2)
    return np.stack([np.cos(theta), -np.sin(theta)]).reshape(2 * n_modes, n_phi)


def eta_tables(cells, owners, n_modes):
    n_eta = cells * owners
    phase = 2.0 * np.pi / n_eta * ((np.arange(n_eta)[None, :] * np.arange(n_modes)[:, None]) % n_eta)
    phase = phase.reshape(n_modes, owners, cells).transpose(0, 2, 1).reshape(n_modes, n_eta)
    cos, sin = np.cos(phase), np.sin(phase)
    forward = np.concatenate([cos, sin]) / math.sqrt(n_eta)
    inverse = np.block([[cos.T, -sin.T], [sin.T, cos.T]]) / math.sqrt(n_modes)
    return forward, inverse


def dot(a, b):
    return jnp.dot(a, b, preferred_element_type=F32)


def dot_rows(a, b):
    return lax.dot_general(a, b, (((1,), (1,)), ((), ())), preferred_element_type=F32)


def split(x):
    high = x.astype(BF16)
    return high, (x - high.astype(F32)).astype(BF16)


def gelu_parts(v):
    square = v * v
    capped = jnp.minimum(square, 27.04)
    poly = -6.666758338545128e-08
    for a in (
        3.1052332348022884e-06, -5.041388393796624e-05, -4.473045135442513e-05,
        0.03634451762350441, 0.7978822527967008,
    ):
        poly = poly * capped + a
    half = 0.5 * jnp.tanh(v * poly)
    density = (1.0 / math.sqrt(2.0 * math.pi)) * jnp.exp2((-0.5 / math.log(2.0)) * square)
    return half, half + v * density


def load(src, dst, sem):
    return pltpu.make_async_copy(src, dst, sem)


def columns(j):
    return pl.ds(pl.multiple_of(j * STEP, STEP), STEP)


def iota(shape, axis):
    return lax.broadcasted_iota(jnp.int32, shape, axis)


def expand_table(chans, width):
    rows, cols = iota((2 * chans, width), 0), iota((2 * chans, width), 1)
    return (rows % chans == cols // chans).astype(F32).astype(BF16)


def spread_table(chans, groups):
    shape = (2 * groups * chans, groups * LANES)
    rows, cols = iota(shape, 0) % (groups * chans), iota(shape, 1)
    same = (rows // chans == cols // LANES) & (rows % chans == cols % chans)
    return same.astype(F32).astype(BF16)


def gather_table(chans, groups):
    shape = (groups * LANES, LANES)
    rows, cols = iota(shape, 0), iota(shape, 1)
    same = (rows // LANES == cols // chans) & (rows % chans == cols % chans)
    return same.astype(F32).astype(BF16)


def collect_table(chans):
    shape = (chans * chans, LANES)
    return (iota(shape, 0) // chans == iota(shape, 1)).astype(F32).astype(BF16)


def pack_spectra(spectra, rows_ref, rows, layers, cells, owners, owned):
    width = spectra.shape[1] // (layers * cells)
    for cell in range(cells):
        for part in range(2):
            pieces = []
            for mode in range(owned):
                top = (part * owned + mode) * owners
                for layer in range(layers):
                    left = (layer * cells + cell) * width
                    pieces.append(spectra[top : top + owners, left : left + width])
            rows_ref[pl.ds(cell * 2 + part, owners, rows), :] = jnp.concatenate(pieces, axis=1)


def xp_kernel(fwd_h, field_h, *refs, sizes):
    layers, cells, owners, owned = sizes
    smalls, out_h, fields, targets, (out, fwd, rows_ref, sems) = refs[:3], refs[3], refs[4:6], refs[6:9], refs[9:]
    half = fields[0].shape[0]
    halves = [(field_h.at[pl.ds(n * half, half), :], fields[n]) for n in range(2)]
    pairs = ((fwd_h, fwd), *halves, *zip(smalls, targets))
    copies = [load(a, b, sems.at[n]) for n, (a, b) in enumerate(pairs)]
    for copy in copies:
        copy.start()
    for copy in copies[:3]:
        copy.wait()
    field = jnp.concatenate([fields[0][...], fields[1][...]], axis=0)
    spectra = dot_rows(fwd[...], field)
    pack_spectra(spectra, rows_ref, 8, layers, cells, owners, owned)
    out[...] = rows_ref[...].reshape(out.shape).astype(BF16)
    send = load(out, out_h, sems.at[len(copies)])
    send.start()
    for copy in (*copies[3:], send):
        copy.wait()


def by_cell(weights, cells):
    rows, cols = weights.shape
    wide = jnp.concatenate([jnp.concatenate([weights] * cells, axis=1)] * cells, axis=0)
    same = iota(wide.shape, 0) // rows == iota(wide.shape, 1) // cols
    return jnp.where(same, wide, 0.0).astype(BF16)


def hidden_kernel(field, w_in, bias, w_out, _, *refs, count, carried):
    sources, (hidden_h, slope_h, base_h), refs = refs[:carried], refs[carried : carried + 3], refs[carried + 3 :]
    targets, refs = refs[:carried], refs[carried:]
    wide_bias, pre, hidden, slope, ins, outs, *own = refs
    base = own[0] if own else base_h
    carries = [load(a, b, ins.at[n]) for n, (a, b) in enumerate(zip(sources, targets))]
    for copy in carries:
        copy.start()
    steps = field.shape[1] // STEP
    chans, hid = w_in.shape
    span = lambda j: pl.ds(j * STEP, STEP)
    pairs = ((hidden, hidden_h), (slope, slope_h), (base, base_h))
    write = lambda n, j: load(
        pairs[n][0].at[:, span(j)], pairs[n][1].at[:, span(j)], outs.at[n, j]
    )
    wide = by_cell(w_in[...].astype(F32).T, count)
    back = by_cell(w_out[...].astype(F32), count)
    wide_bias[...] = jnp.broadcast_to(bias[...].T, wide_bias.shape)

    def project(j):
        base[:, span(j)] = dot(back, hidden[:, span(j)])
        if own:
            write(2, j).start()

    for j in range(steps):
        pre[:, span(j)] = dot(wide, field[:, span(j)])
        if j:
            project(j - 1)
        for left in range(j * STEP, (j + 1) * STEP, CHUNK):
            at = slice(left, left + CHUNK)
            for i in range(count):
                tall = slice(i * hid, (i + 1) * hid)
                v = pre[tall, at] + wide_bias[...]
                half, centred = gelu_parts(v)
                hidden[tall, at] = (v * (0.5 + half)).astype(BF16)
                slope[tall, at] = centred.astype(BF16)
        for n in range(2):
            write(n, j).start()
    project(steps - 1)
    for j in range(steps):
        for n in range(3 if own else 2):
            write(n, j).wait()
    for copy in carries:
        copy.wait()


def unpack(blocks, rows_ref, cells, owners):
    rows = blocks.shape[1]
    rows_ref[...] = blocks[...].astype(F32).reshape(rows_ref.shape)
    part = lambda p: jnp.concatenate(
        [rows_ref[pl.ds(cell * 2 + p, owners, rows), :] for cell in range(cells)], axis=0
    )
    return jnp.concatenate([part(0), part(1)], axis=1).astype(BF16)


def modes_of(spectra, forward):
    both = dot(forward[...], spectra)
    half = both.shape[0] // 2
    real = both[:half, :LANES] + both[half:, LANES:]
    imag = both[:half, LANES:] - both[half:, :LANES]
    return jnp.concatenate([real, imag], axis=0)


def fields_of(modes, inverse, rows_ref, rows, cells, owners):
    high, low = split(modes)
    fields = dot(inverse[...], jnp.concatenate([high, low, high], axis=0))
    for part in range(2):
        for cell in range(cells):
            top = (part * cells + cell) * owners
            rows_ref[pl.ds(cell * 2 + part, owners, rows), :] = fields[top : top + owners]


def widen(modes, pick, chans):
    high, low = split(modes[:, pick * chans : (pick + 1) * chans])
    return jnp.concatenate([high, low], axis=1)


def mix_kernel(
    blocks, weights, forward, inverse, out_h, modes_h, out, modes, rows_ref, sems, *, sizes,
):
    layers, cells, owners, owned = sizes
    chans = LANES // (layers * owned)
    expand = expand_table(chans, chans * chans)
    gather = gather_table(chans, layers * owned)
    spectra = unpack(blocks, rows_ref, cells, owners)
    z = modes_of(spectra, forward)
    modes[...] = z
    save = load(modes, modes_h, sems.at[0])
    save.start()
    half = z.shape[0] // 2
    groups = []
    for mode in range(owned):
        wide = jnp.concatenate(
            [widen(z, mode * layers + layer, chans) for layer in range(layers)], axis=0
        )
        sums = [[None, None] for _ in range(layers)]
        for left in range(0, weights.shape[3], CHUNK):
            wr = weights[0, mode, :, left : left + CHUNK].astype(F32)
            wi = weights[1, mode, :, left : left + CHUNK].astype(F32)
            x = dot(wide, expand[:, left : left + CHUNK])
            for layer in range(layers):
                top = 2 * layer * half
                xr, xi = x[top : top + half], x[top + half : top + 2 * half]
                for part, t in enumerate((xr * wr - xi * wi, xr * wi + xi * wr)):
                    t = t[:, :LANES] + t[:, LANES:]
                    old = sums[layer][part]
                    sums[layer][part] = t if old is None else old + t
        groups += [jnp.concatenate(pair, axis=0) for pair in sums]
    high, low = split(jnp.concatenate(groups, axis=1))
    mixed = dot(high, gather) + dot(low, gather)
    fields_of(mixed, inverse, rows_ref, 8, cells, owners)
    out[...] = rows_ref[...].reshape(out.shape).astype(BF16)
    send = load(out, out_h, sems.at[1])
    send.start()
    save.wait()
    send.wait()


def phi_rows(blocks, rows_ref, layers, cells, owners, owned):
    rows = blocks.shape[1]
    rows_ref[...] = blocks[...].astype(F32).reshape(rows_ref.shape)
    chans = LANES // (layers * owned)
    tall = []
    for part in range(2):
        line = [rows_ref[pl.ds(cell * 2 + part, owners, rows), :] for cell in range(cells)]
        for mode in range(owned):
            pieces = []
            for layer in range(layers):
                left = (mode * layers + layer) * chans
                pieces += [line[cell][:, left : left + chans] for cell in range(cells)]
            tall.append(jnp.concatenate(pieces, axis=1))
    return jnp.concatenate(tall, axis=0).T.astype(BF16)


def gpre_kernel(
    blocks, cot, base_a, inv, w_out, field_h, hidden_a, hidden_b, slope_a, slope_b, base_h,
    fwd_h, out_h, grad_h,
    out, field, hidden, slope, base_b, fwd, gpre, grad_b, waves, back, pre, grad,
    rows_in, rows_out, slab, ins, outs, *, sizes,
):
    layers, cells, owners, owned = sizes
    n_phi = field.shape[1]
    chans, hid = w_out.shape
    thin, tall = base_a.shape[0], hidden_a.shape[0]
    count = thin // chans
    rows = lambda n: pl.ds(n * thin, thin)
    high = lambda n: pl.ds(n * tall, tall)
    bases = (base_a, base_b)
    others = [load(fwd_h, fwd, ins.at[2, 0]), load(base_h, base_b, ins.at[2, 1])]
    slopes = [
        load((slope_a, slope_b)[n], slope.at[high(n), :], ins.at[n, 0]) for n in range(2)
    ]
    late = [
        [
            load((hidden_a, hidden_b)[n], hidden.at[high(n), :], ins.at[n, 1]),
            load(field_h.at[rows(n), :], field.at[rows(n), :], ins.at[n, 2]),
        ]
        for n in range(2)
    ]
    writes = [load(grad_b.at[high(n), :], grad_h.at[high(n), :], outs.at[n]) for n in range(2)]
    for copy in (slopes[0], others[1], others[0], *late[0], slopes[1], *late[1]):
        copy.start()
    waves[...] = phi_rows(blocks, rows_in, layers, cells, owners, owned)
    back[...] = by_cell(w_out[...].astype(F32).T, count)

    def products(n):
        here, up = slice(n * thin, (n + 1) * thin), slice(n * tall, (n + 1) * tall)
        spectra = dot_rows(fwd[...], gpre[here, :])
        part_out = dot_rows(hidden[up, :], gpre[here, :])
        part_in = dot_rows(grad_b[up, :], field[here, :])
        diagonal = lambda x: sum(
            x[i * hid : (i + 1) * hid, i * chans : (i + 1) * chans] for i in range(count)
        )
        return spectra, diagonal(part_in), diagonal(part_out)

    total = jnp.zeros((hid, LANES), F32)
    results = []
    for n in range(2):
        here, up = slice(n * thin, (n + 1) * thin), slice(n * tall, (n + 1) * tall)
        pre[here, :] = dot(waves[here, :], inv[...])
        if n:
            for copy in (*others, *late[0], slopes[1]):
                copy.wait()
            results.append(products(0))
        for left in range(0, n_phi, CHUNK):
            at = slice(left, left + CHUNK)
            for top in range(here.start, here.stop, hid):
                tile = slice(top, top + hid)
                base = bases[n][top - here.start : top - here.start + hid, at]
                g = 0.5 + gelu_parts(pre[tile, at] + base)[1]
                gpre[tile, at] = (cot[tile, at].astype(F32) * g).astype(BF16)
        for left in range(0, n_phi, STEP):
            grad[up, left : left + STEP] = dot(back[...], gpre[here, left : left + STEP])
        if n == 0:
            slopes[0].wait()
        for left in range(0, n_phi, CHUNK):
            at = slice(left, left + CHUNK)
            for top in range(up.start, up.stop, hid):
                tile = slice(top, top + hid)
                g = grad[tile, at] * (0.5 + slope[tile, at].astype(F32))
                grad_b[tile, at] = g.astype(BF16)
                total = total + (g[:, :LANES] + g[:, LANES:])
        writes[n].start()
    for copy in late[1]:
        copy.wait()
    results.append(products(1))
    spectra = jnp.concatenate([r[0] for r in results], axis=1)
    pack_spectra(spectra, rows_out, 16, layers, cells, owners, owned)
    part_in, part_out = results[0][1] + results[1][1], results[0][2] + results[1][2]
    bias = jnp.sum(total, axis=1, keepdims=True)
    zeros = jnp.zeros((hid, LANES - 2 * chans), F32)
    full = jnp.concatenate([part_in, part_out, zeros], axis=1)
    full = jnp.where(iota((hid, LANES), 1) == 2 * chans, bias, full)
    high = full.astype(BF16).astype(F32)
    each = hid // owners
    for at, value in enumerate((high, full - high)):
        slab[...] = value
        for row in range(each):
            rows_out[pl.ds(8 + at * each + row, owners, 16), :] = slab[pl.ds(row, owners, each), :]
    for row in range(8 + 2 * each, 16):
        rows_out[pl.ds(row, owners, 16), :] = jnp.zeros((owners, LANES), F32)
    out[...] = rows_out[...].reshape(out.shape).astype(BF16)
    writes.append(load(out, out_h, outs.at[2]))
    writes[2].start()
    for write in writes:
        write.wait()


def mlp_grad_kernel(cot_h, grad_h, w_in_h, *refs, count, carried):
    sources, out, targets, refs = refs[:carried], refs[carried], refs[carried + 1 : 2 * carried + 1], refs[2 * carried + 1 :]
    cot, grad_b, w_in, sems = refs
    chans, hid = w_in.shape
    half = cot.shape[0] // 2
    copies = [load(w_in_h, w_in, sems.at[0])]
    for n in range(2):
        low, high = pl.ds(n * half, half), pl.ds(n * half // chans * hid, half // chans * hid)
        copies.append(load(cot_h.at[low, :], cot.at[low, :], sems.at[1 + 2 * n]))
        copies.append(load(grad_h.at[high, :], grad_b.at[high, :], sems.at[2 + 2 * n]))
    copies += [load(a, b, sems.at[5 + n]) for n, (a, b) in enumerate(zip(sources, targets))]
    for copy in copies:
        copy.start()
    copies[0].wait()
    weights = by_cell(w_in[...].astype(F32), count)
    for n in range(2):
        for copy in copies[1 + 2 * n : 3 + 2 * n]:
            copy.wait()
        low = slice(n * half, (n + 1) * half)
        high = slice(low.start // chans * hid, low.stop // chans * hid)
        for left in range(0, cot.shape[1], STEP):
            at = slice(left, left + STEP)
            out[low, at] = cot[low, at].astype(F32) + dot(weights, grad_b[high, at])
    for copy in copies[5:]:
        copy.wait()


def back_kernel(
    blocks, weights, forward, inverse, _, out_h, modes_h, out, modes, rows_ref, sems, *, sizes, each,
):
    layers, cells, owners, owned = sizes
    chans = LANES // (layers * owned)
    spread = spread_table(chans, layers * owned)
    collect = collect_table(chans)
    spectra = unpack(blocks, rows_ref, cells, owners)
    z = modes_of(spectra, forward)
    modes[...] = z
    save = load(modes, modes_h, sems.at[0])
    save.start()
    totals = []
    for row in range(each):
        at = 8 + row
        total = jnp.sum(
            rows_ref[pl.ds(at, owners, 16), :] + rows_ref[pl.ds(at + each, owners, 16), :],
            axis=0,
            keepdims=True,
        )
        totals.append(total)
    half = z.shape[0] // 2
    high, low = split(z)
    wide = dot(jnp.concatenate([high, low], axis=1), spread)
    pieces = []
    for mode in range(owned):
        acc = None
        for left in range(0, weights.shape[3], CHUNK):
            wr = weights[0, mode, :, left : left + CHUNK].astype(F32)
            wi = weights[1, mode, :, left : left + CHUNK].astype(F32)
            terms = []
            for layer in range(layers):
                pick = (mode * layers + layer) * LANES
                g = jnp.concatenate([wide[:, pick : pick + LANES]] * (CHUNK // LANES), axis=1)
                gr, gi = g[:half], g[half:]
                terms += [(gr * wr + gi * wi).astype(BF16), (gi * wr - gr * wi).astype(BF16)]
            s = dot(jnp.concatenate(terms, axis=0), collect[left : left + CHUNK, :])
            acc = s if acc is None else acc + s
        acc = [acc[2 * n * half : 2 * (n + 1) * half] for n in range(layers)]
        pieces += [a[:, :chans] for a in acc]
    fields_of(jnp.concatenate(pieces, axis=1), inverse, rows_ref, 16, cells, owners)
    for row, total in enumerate(totals):
        high = total.astype(BF16).astype(F32)
        rows_ref[pl.ds(8 + row, owners, 16), :] = jnp.broadcast_to(high, (owners, LANES))
        rows_ref[pl.ds(8 + each + row, owners, 16), :] = jnp.broadcast_to(total - high, (owners, LANES))
    out[...] = rows_ref[...].reshape(out.shape).astype(BF16)
    send = load(out, out_h, sems.at[1])
    send.start()
    save.wait()
    send.wait()


def weight_grad_kernel(zx_h, zg_h, out_h, zx, zg, out, sems, *, sizes, factor):
    layers, owned = sizes[0], sizes[3]
    chans = LANES // (layers * owned)
    copies = [load(a, b, sems.at[n]) for n, (a, b) in enumerate(((zx_h, zx), (zg_h, zg)))]
    for copy in copies:
        copy.start()
    expand = expand_table(chans, chans * chans)
    spread = spread_table(chans, layers * owned)
    for copy in copies:
        copy.wait()
    z = zx[...] * factor
    half = z.shape[0] // 2
    high, low = split(zg[...])
    wide = dot(jnp.concatenate([high, low], axis=1), spread)
    saves = []
    for mode in range(owned):
        split_z = [widen(z, mode * layers + layer, chans) for layer in range(layers)]
        for left in range(0, out.shape[3], CHUNK):
            real = imag = 0.0
            for layer in range(layers):
                x = dot(split_z[layer], expand[:, left : left + CHUNK])
                xr, xi = x[:half], x[half:]
                pick = (mode * layers + layer) * LANES
                g = jnp.concatenate([wide[:, pick : pick + LANES]] * (CHUNK // LANES), axis=1)
                gr, gi = g[:half], g[half:]
                real = real + (xr * gr + xi * gi)
                imag = imag + (xr * gi - xi * gr)
            out[0, mode, :, left : left + CHUNK] = real
            out[1, mode, :, left : left + CHUNK] = imag
        for part in range(2):
            saves.append(
                load(out.at[part, mode], out_h.at[part, mode], sems.at[2 + part * owned + mode])
            )
            saves[-1].start()
    for save in saves:
        save.wait()


def final_kernel(
    blocks, base, inv, _, out_h, in_h, out_w_h, bias_h, out, rows_ref, slab, turned, outs, *, sizes, norm,
):
    layers, cells, owners, owned = sizes
    chans = in_h.shape[0]
    count = 4
    span = base.shape[0] // count
    waves = phi_rows(blocks, rows_ref, layers, cells, owners, owned)
    hid = slab.shape[0]
    each = hid // owners
    for row in range(each):
        slab[pl.ds(row, owners, each), :] = (
            rows_ref[pl.ds(8 + row, owners, 16), :] + rows_ref[pl.ds(8 + each + row, owners, 16), :]
        ) * norm
    turned[...] = slab[...].T
    writes = [
        load(turned.at[pl.ds(n * chans, h.shape[0]), :], h, outs.at[1, n])
        for n, h in enumerate((in_h, out_w_h, bias_h))
    ]
    for write in writes:
        write.start()
    for j in range(count):
        here, rows = slice(j * span, (j + 1) * span), pl.ds(j * span, span)
        for left in range(0, base.shape[1], STEP):
            at = slice(left, left + STEP)
            out[here, at] = base[here, at] + dot(waves[here], inv[:, at])
        writes.append(load(out.at[rows, :], out_h.at[rows, :], outs.at[0, j]))
        writes[-1].start()
    for write in writes:
        write.wait()


def call(kernel, ins, outs, scratch, flops, *args, **static):
    space = {"h": pltpu.HBM, "v": pltpu.VMEM, "w": pltpu.VMEM}
    keep = {"h": pltpu.HBM, "w": pltpu.VMEM}
    shapes = [jax.ShapeDtypeStruct(s, d) for _, s, d in outs]
    size = lambda x: math.prod(x.shape) * x.dtype.itemsize
    moved = sum(size(x) for x in (*args, *shapes))
    args = [
        pltpu.with_memory_space_constraint(x, keep[k]) if k in keep else x
        for k, x in zip(ins, args)
    ]
    return pl.pallas_call(
        functools.partial(kernel, **static),
        out_shape=[
            keep[o[0]](x.shape, x.dtype) if o[0] in keep else x for o, x in zip(outs, shapes)
        ],
        in_specs=[pl.BlockSpec(memory_space=space[k]) for k in ins],
        out_specs=[pl.BlockSpec(memory_space=space[k]) for k, _, _ in outs],
        scratch_shapes=[
            pltpu.SemaphoreType.DMA(s) if d is None else pltpu.VMEM(s, d) for s, d in scratch
        ],
        compiler_params=pltpu.CompilerParams(vmem_limit_bytes=LIMIT),
        cost_estimate=pl.CostEstimate(
            flops=flops,
            bytes_accessed=moved,
            transcendentals=0,
        ),
    )(*args)


def local(field_in, grad_out, spectral_weight, mlp_in, mlp_bias, mlp_out):
    layers, cells, chans, n_phi = field_in.shape
    owners = lax.axis_size("eta")
    depth = lax.axis_size("depth")
    n_eta = cells * owners
    owned = spectral_weight.shape[1]
    n_eta_modes = spectral_weight.shape[2]
    n_phi_modes = owned * owners
    hid = mlp_in.shape[1]
    count = layers * cells
    each = hid // owners
    sizes = (layers, cells, owners, owned)
    pairs = phi_pairs(n_phi, owned, owners)
    phi_fwd = jnp.asarray(pairs / math.sqrt(n_phi), BF16)
    phi_inv = jnp.asarray(pairs / math.sqrt(n_phi_modes), BF16)
    forward, inverse = eta_tables(cells, owners, n_eta_modes)
    forward = jnp.asarray(forward, BF16)
    inverse_high = inverse.astype(BF16)
    inverse_low = (inverse - inverse_high.astype(np.float64)).astype(BF16)
    inverse = jnp.asarray(np.concatenate([inverse_high, inverse_high, inverse_low], axis=1))

    thin = (count * chans, n_phi)
    tall = (count * hid, n_phi)
    field = field_in.reshape(thin)
    cot = grad_out.reshape(thin)
    w_out = mlp_out.T
    steps = n_phi // STEP
    exchange = lambda x: lax.all_to_all(x, "eta", 0, 0, tiled=True)
    small = (owners, 8, LANES)
    large = (owners, 16, LANES)
    modes = (2 * n_eta_modes, LANES)
    small_rows = ((owners * 8, LANES), F32)
    large_rows = ((owners * 16, LANES), F32)
    table = ((2 * n_phi_modes, n_phi), BF16)
    grid_mul = 2 * count * n_phi * chans

    smalls = (mlp_in, mlp_bias[None], w_out)
    mixing = (spectral_weight, forward, inverse)
    half = count // 2
    half_thin = (half * chans, n_phi)
    xp, field_a, field_b, w_in_v, bias_v, w_out_v = call(
        xp_kernel, "hhhhh",
        [("h", small, BF16), *[("w", half_thin, BF16)] * 2, *(("w", x.shape, x.dtype) for x in smalls)],
        [(small, BF16), table, small_rows, ((7,), None)],
        grid_mul * 2 * n_phi_modes, phi_fwd, field, *smalls, sizes=sizes,
    )
    xp = exchange(xp)
    part = (half * hid, n_phi)

    def hidden_half(field, after, keep_base, *carried):
        return call(
            hidden_kernel, "wwwwh" + "h" * len(carried),
            [
                ("h", part, BF16), ("h", part, BF16), (keep_base, half_thin, F32),
                *(("w", x.shape, x.dtype) for x in carried),
            ],
            [
                ((hid, CHUNK), F32), (part, F32), (part, BF16), (part, BF16),
                ((len(carried),), None), ((3, steps), None),
                *([(half_thin, F32)] if keep_base == "h" else []),
            ],
            grid_mul * hid, field, w_in_v, bias_v, w_out_v, after, *carried,
            count=half, carried=len(carried),
        )

    hidden_a, slope_a, base_a, weights, forward, inverse = hidden_half(
        field_a, w_out, "w", *mixing
    )
    wx, zx = call(
        mix_kernel, "vwww", [("h", small, BF16), ("h", modes, F32)],
        [(small, BF16), (modes, F32), small_rows, ((2,), None)],
        1 << 24, xp, weights, forward, inverse, sizes=sizes,
    )
    wx = exchange(wx)
    hidden_b, slope_b, base_b, cot_v, inv_v = hidden_half(field_b, zx, "h", cot, phi_inv)
    gp, hidden_gb = call(
        gpre_kernel, "vwwwwhhhhhhh", [("h", large, BF16), ("h", tall, BF16)],
        [
            (large, BF16), (thin, BF16), (tall, BF16), (tall, BF16), (half_thin, F32), table,
            (thin, BF16), (tall, BF16),
            ((count * chans, 2 * n_phi_modes), BF16), ((half * hid, half * chans), BF16),
            (thin, F32), (tall, F32), small_rows, large_rows, ((hid, LANES), F32),
            ((3, 3), None), ((3,), None),
        ],
        grid_mul * (4 * n_phi_modes + 4 * hid), wx, cot_v, base_a, inv_v, w_out_v,
        field, hidden_a, hidden_b, slope_a, slope_b, base_b, phi_fwd, sizes=sizes,
    )
    gp = exchange(gp)
    carried = (phi_inv, *mixing)
    partial, inverse_phi, weights, forward, inverse = call(
        mlp_grad_kernel, "hhh" + "h" * len(carried),
        [("w", thin, F32), *(("w", x.shape, x.dtype) for x in carried)],
        [(thin, BF16), (tall, BF16), (mlp_in.shape, BF16), ((5 + len(carried),), None)],
        grid_mul * hid, cot, hidden_gb, mlp_in, *carried, count=half, carried=len(carried),
    )
    wb, zg = call(
        back_kernel, "vwwww", [("h", large, BF16), ("h", modes, F32)],
        [(large, BF16), (modes, F32), large_rows, ((2,), None)],
        1 << 24, gp, weights, forward, inverse, partial, sizes=sizes, each=each,
    )
    wb = exchange(wb)
    factor = math.sqrt(n_phi * n_eta / (n_phi_modes * n_eta_modes))
    grad_shape = (2, owned, n_eta_modes, chans * chans)
    (grad_spectral,) = call(
        weight_grad_kernel, "hh", [("h", grad_shape, F32)],
        [(modes, F32), (modes, F32), (grad_shape, F32), ((2 + 2 * owned,), None)],
        1 << 24, zx, zg, sizes=sizes, factor=factor,
    )
    norm = 1.0 / math.sqrt(layers * depth * n_eta * n_phi)
    grad_in, total_in, total_out, total_bias = call(
        final_kernel, "vwwh",
        [("h", thin, F32), ("h", (chans, hid), F32), ("h", (chans, hid), F32), ("h", (1, hid), F32)],
        [
            (thin, F32), large_rows, ((hid, LANES), F32), ((LANES, hid), F32), ((2, 4), None),
        ],
        grid_mul * 2 * n_phi_modes, wb, partial, inverse_phi, grad_spectral, sizes=sizes, norm=norm,
    )
    if depth > 1:
        grad_spectral = lax.psum_scatter(grad_spectral, "depth", scatter_dimension=2, tiled=True)
        total_in, total_out, total_bias = lax.psum((total_in, total_out, total_bias), "depth")
    return (grad_in.reshape(field_in.shape), grad_spectral, total_in, total_out.T, total_bias[0])


def solution(mesh):
    return jax.shard_map(
        local,
        mesh=mesh,
        in_specs=(
            P("depth", "eta", None, None),
            P("depth", "eta", None, None),
            P(None, "eta", None, None),
            P(),
            P(),
            P(),
        ),
        out_specs=(P("depth", "eta", None, None), P(None, "eta", "depth", None), P(), P(), P()),
        check_vma=False,
    )
```

```python
import functools
import math

import jax
import jax.numpy as jnp
import numpy as np
from jax import lax
from jax.experimental import pallas as pl
from jax.experimental.pallas import tpu as pltpu
from jax.sharding import PartitionSpec as P

F32 = jnp.float32
BF16 = jnp.bfloat16
LANES = 128
CHUNK = 256
STEP = 512
LIMIT = 32 * 1024 * 1024


def phi_pairs(n_phi, owned, owners):
    n_modes = owned * owners
    index = np.arange(n_modes)
    freq = np.where(index < n_modes // 2, index, n_phi - n_modes + index)
    theta = 2.0 * np.pi / n_phi * ((np.arange(n_phi)[None, :] * freq[:, None]) % n_phi)
    theta = theta.reshape(owners, owned, n_phi).transpose(1, 0, 2)
    return np.stack([np.cos(theta), -np.sin(theta)]).reshape(2 * n_modes, n_phi)


def eta_tables(cells, owners, n_modes):
    n_eta = cells * owners
    phase = 2.0 * np.pi / n_eta * ((np.arange(n_eta)[None, :] * np.arange(n_modes)[:, None]) % n_eta)
    phase = phase.reshape(n_modes, owners, cells).transpose(0, 2, 1).reshape(n_modes, n_eta)
    cos, sin = np.cos(phase), np.sin(phase)
    forward = np.concatenate([cos, sin]) / math.sqrt(n_eta)
    inverse = np.block([[cos.T, -sin.T], [sin.T, cos.T]]) / math.sqrt(n_modes)
    return forward, inverse


def dot(a, b):
    return jnp.dot(a, b, preferred_element_type=F32)


def dot_rows(a, b):
    return lax.dot_general(a, b, (((1,), (1,)), ((), ())), preferred_element_type=F32)


def split(x):
    high = x.astype(BF16)
    return high, (x - high.astype(F32)).astype(BF16)


def gelu_parts(v):
    square = v * v
    capped = jnp.minimum(square, 27.04)
    poly = -6.666758338545128e-08
    for a in (
        3.1052332348022884e-06, -5.041388393796624e-05, -4.473045135442513e-05,
        0.03634451762350441, 0.7978822527967008,
    ):
        poly = poly * capped + a
    half = 0.5 * jnp.tanh(v * poly)
    density = (1.0 / math.sqrt(2.0 * math.pi)) * jnp.exp2((-0.5 / math.log(2.0)) * square)
    return half, half + v * density


def load(src, dst, sem):
    return pltpu.make_async_copy(src, dst, sem)


def columns(j):
    return pl.ds(pl.multiple_of(j * STEP, STEP), STEP)


def iota(shape, axis):
    return lax.broadcasted_iota(jnp.int32, shape, axis)


def expand_table(chans, width):
    rows, cols = iota((2 * chans, width), 0), iota((2 * chans, width), 1)
    return (rows % chans == cols // chans).astype(F32).astype(BF16)


def spread_table(chans, groups):
    shape = (2 * groups * chans, groups * LANES)
    rows, cols = iota(shape, 0) % (groups * chans), iota(shape, 1)
    same = (rows // chans == cols // LANES) & (rows % chans == cols % chans)
    return same.astype(F32).astype(BF16)


def gather_table(chans, groups):
    shape = (groups * LANES, LANES)
    rows, cols = iota(shape, 0), iota(shape, 1)
    same = (rows // LANES == cols // chans) & (rows % chans == cols % chans)
    return same.astype(F32).astype(BF16)


def collect_table(chans):
    shape = (chans * chans, LANES)
    return (iota(shape, 0) // chans == iota(shape, 1)).astype(F32).astype(BF16)


def pack_spectra(spectra, rows_ref, rows, layers, cells, owners, owned):
    width = spectra.shape[1] // (layers * cells)
    for cell in range(cells):
        for part in range(2):
            pieces = []
            for mode in range(owned):
                top = (part * owned + mode) * owners
                for layer in range(layers):
                    left = (layer * cells + cell) * width
                    pieces.append(spectra[top : top + owners, left : left + width])
            rows_ref[pl.ds(cell * 2 + part, owners, rows), :] = jnp.concatenate(pieces, axis=1)


def xp_kernel(fwd_h, field_h, *refs, sizes):
    layers, cells, owners, owned = sizes
    smalls, out_h, fields, targets, (out, fwd, rows_ref, sems) = refs[:3], refs[3], refs[4:6], refs[6:9], refs[9:]
    half = fields[0].shape[0]
    halves = [(field_h.at[pl.ds(n * half, half), :], fields[n]) for n in range(2)]
    pairs = ((fwd_h, fwd), *halves, *zip(smalls, targets))
    copies = [load(a, b, sems.at[n]) for n, (a, b) in enumerate(pairs)]
    for copy in copies:
        copy.start()
    for copy in copies[:3]:
        copy.wait()
    field = jnp.concatenate([fields[0][...], fields[1][...]], axis=0)
    spectra = dot_rows(fwd[...], field)
    pack_spectra(spectra, rows_ref, 8, layers, cells, owners, owned)
    out[...] = rows_ref[...].reshape(out.shape).astype(BF16)
    send = load(out, out_h, sems.at[len(copies)])
    send.start()
    for copy in (*copies[3:], send):
        copy.wait()


def by_cell(weights, cells):
    rows, cols = weights.shape
    wide = jnp.concatenate([jnp.concatenate([weights] * cells, axis=1)] * cells, axis=0)
    same = iota(wide.shape, 0) // rows == iota(wide.shape, 1) // cols
    return jnp.where(same, wide, 0.0).astype(BF16)


def hidden_kernel(field, w_in, bias, w_out, _, *refs, count, carried):
    sources, (hidden_h, slope_h, base_h), refs = refs[:carried], refs[carried : carried + 3], refs[carried + 3 :]
    targets, refs = refs[:carried], refs[carried:]
    wide_bias, pre, hidden, slope, ins, outs, *own = refs
    base = own[0] if own else base_h
    carries = [load(a, b, ins.at[n]) for n, (a, b) in enumerate(zip(sources, targets))]
    for copy in carries:
        copy.start()
    steps = field.shape[1] // STEP
    chans, hid = w_in.shape
    span = lambda j: pl.ds(j * STEP, STEP)
    pairs = ((hidden, hidden_h), (slope, slope_h), (base, base_h))
    write = lambda n, j: load(
        pairs[n][0].at[:, span(j)], pairs[n][1].at[:, span(j)], outs.at[n, j]
    )
    wide = by_cell(w_in[...].astype(F32).T, count)
    back = by_cell(w_out[...].astype(F32), count)
    wide_bias[...] = jnp.broadcast_to(bias[...].T, wide_bias.shape)

    def project(j):
        base[:, span(j)] = dot(back, hidden[:, span(j)])
        if own:
            write(2, j).start()

    for j in range(steps):
        pre[:, span(j)] = dot(wide, field[:, span(j)])
        if j:
            project(j - 1)
        for left in range(j * STEP, (j + 1) * STEP, CHUNK):
            at = slice(left, left + CHUNK)
            for i in range(count):
                tall = slice(i * hid, (i + 1) * hid)
                v = pre[tall, at] + wide_bias[...]
                half, centred = gelu_parts(v)
                hidden[tall, at] = (v * (0.5 + half)).astype(BF16)
                slope[tall, at] = centred.astype(BF16)
        for n in range(2):
            write(n, j).start()
    project(steps - 1)
    for j in range(steps):
        for n in range(3 if own else 2):
            write(n, j).wait()
    for copy in carries:
        copy.wait()


def unpack(blocks, rows_ref, cells, owners):
    rows = rows_ref.shape[0] // owners
    rows_ref[...] = blocks[...].astype(F32).reshape(rows_ref.shape)
    part = lambda p: jnp.concatenate(
        [rows_ref[pl.ds(cell * 2 + p, owners, rows), :] for cell in range(cells)], axis=0
    )
    return jnp.concatenate([part(0), part(1)], axis=1).astype(BF16)


def modes_of(spectra, forward):
    both = dot(forward[...], spectra)
    half = both.shape[0] // 2
    real = both[:half, :LANES] + both[half:, LANES:]
    imag = both[:half, LANES:] - both[half:, :LANES]
    return jnp.concatenate([real, imag], axis=0)


def fields_of(modes, inverse, rows_ref, rows, cells, owners):
    high, low = split(modes)
    fields = dot(inverse[...], jnp.concatenate([high, low, high], axis=0))
    for part in range(2):
        for cell in range(cells):
            top = (part * cells + cell) * owners
            rows_ref[pl.ds(cell * 2 + part, owners, rows), :] = fields[top : top + owners]


def widen(modes, pick, chans):
    high, low = split(modes[:, pick * chans : (pick + 1) * chans])
    return jnp.concatenate([high, low], axis=1)


def mix_kernel(
    blocks, weights, forward, inverse, out_h, modes_h, out, modes, rows_ref, sems, *, sizes,
):
    layers, cells, owners, owned = sizes
    chans = LANES // (layers * owned)
    expand = expand_table(chans, chans * chans)
    gather = gather_table(chans, layers * owned)
    spectra = unpack(blocks, rows_ref, cells, owners)
    z = modes_of(spectra, forward)
    modes[...] = z
    save = load(modes, modes_h, sems.at[0])
    save.start()
    half = z.shape[0] // 2
    groups = []
    for mode in range(owned):
        wide = jnp.concatenate(
            [widen(z, mode * layers + layer, chans) for layer in range(layers)], axis=0
        )
        sums = [[None, None] for _ in range(layers)]
        for left in range(0, weights.shape[3], CHUNK):
            wr = weights[0, mode, :, left : left + CHUNK].astype(F32)
            wi = weights[1, mode, :, left : left + CHUNK].astype(F32)
            x = dot(wide, expand[:, left : left + CHUNK])
            for layer in range(layers):
                top = 2 * layer * half
                xr, xi = x[top : top + half], x[top + half : top + 2 * half]
                for part, t in enumerate((xr * wr - xi * wi, xr * wi + xi * wr)):
                    t = t[:, :LANES] + t[:, LANES:]
                    old = sums[layer][part]
                    sums[layer][part] = t if old is None else old + t
        groups += [jnp.concatenate(pair, axis=0) for pair in sums]
    high, low = split(jnp.concatenate(groups, axis=1))
    mixed = dot(high, gather) + dot(low, gather)
    fields_of(mixed, inverse, rows_ref, 8, cells, owners)
    out[...] = rows_ref[...].reshape(out.shape).astype(BF16)
    send = load(out, out_h, sems.at[1])
    send.start()
    save.wait()
    send.wait()


def phi_rows(blocks, rows_ref, layers, cells, owners, owned):
    rows = rows_ref.shape[0] // owners
    rows_ref[...] = blocks[...].astype(F32).reshape(rows_ref.shape)
    chans = LANES // (layers * owned)
    tall = []
    for part in range(2):
        line = [rows_ref[pl.ds(cell * 2 + part, owners, rows), :] for cell in range(cells)]
        for mode in range(owned):
            pieces = []
            for layer in range(layers):
                left = (mode * layers + layer) * chans
                pieces += [line[cell][:, left : left + chans] for cell in range(cells)]
            tall.append(jnp.concatenate(pieces, axis=1))
    return jnp.concatenate(tall, axis=0).T.astype(BF16)


def gpre_kernel(
    blocks, cot, base_a, inv, w_out, field_h, hidden_a, hidden_b, slope_a, slope_b, base_h,
    fwd_h, out_h, grad_h,
    out, field, hidden, slope, base_b, fwd, gpre, grad_b, waves, back, pre, grad,
    rows_in, rows_out, slab, ins, outs, *, sizes,
):
    layers, cells, owners, owned = sizes
    n_phi = field.shape[1]
    chans, hid = w_out.shape
    thin, tall = base_a.shape[0], hidden_a.shape[0]
    count = thin // chans
    rows = lambda n: pl.ds(n * thin, thin)
    high = lambda n: pl.ds(n * tall, tall)
    bases = (base_a, base_b)
    others = [load(fwd_h, fwd, ins.at[2, 0]), load(base_h, base_b, ins.at[2, 1])]
    slopes = [
        load((slope_a, slope_b)[n], slope.at[high(n), :], ins.at[n, 0]) for n in range(2)
    ]
    late = [
        [
            load((hidden_a, hidden_b)[n], hidden.at[high(n), :], ins.at[n, 1]),
            load(field_h.at[rows(n), :], field.at[rows(n), :], ins.at[n, 2]),
        ]
        for n in range(2)
    ]
    writes = [load(grad_b.at[high(n), :], grad_h.at[high(n), :], outs.at[n]) for n in range(2)]
    for copy in (slopes[0], others[1], others[0], *late[0], slopes[1], *late[1]):
        copy.start()
    waves[...] = phi_rows(blocks, rows_in, layers, cells, owners, owned)
    back[...] = by_cell(w_out[...].astype(F32).T, count)

    def products(n):
        here, up = slice(n * thin, (n + 1) * thin), slice(n * tall, (n + 1) * tall)
        spectra = dot_rows(fwd[...], gpre[here, :])
        part_out = dot_rows(hidden[up, :], gpre[here, :])
        part_in = dot_rows(grad_b[up, :], field[here, :])
        diagonal = lambda x: sum(
            x[i * hid : (i + 1) * hid, i * chans : (i + 1) * chans] for i in range(count)
        )
        return spectra, diagonal(part_in), diagonal(part_out)

    total = jnp.zeros((hid, LANES), F32)
    results = []
    for n in range(2):
        here, up = slice(n * thin, (n + 1) * thin), slice(n * tall, (n + 1) * tall)
        pre[here, :] = dot(waves[here, :], inv[...])
        if n:
            for copy in (*others, *late[0], slopes[1]):
                copy.wait()
            results.append(products(0))
        for left in range(0, n_phi, CHUNK):
            at = slice(left, left + CHUNK)
            for top in range(here.start, here.stop, hid):
                tile = slice(top, top + hid)
                base = bases[n][top - here.start : top - here.start + hid, at]
                g = 0.5 + gelu_parts(pre[tile, at] + base)[1]
                gpre[tile, at] = (cot[tile, at].astype(F32) * g).astype(BF16)
        for left in range(0, n_phi, STEP):
            grad[up, left : left + STEP] = dot(back[...], gpre[here, left : left + STEP])
        if n == 0:
            slopes[0].wait()
        for left in range(0, n_phi, CHUNK):
            at = slice(left, left + CHUNK)
            for top in range(up.start, up.stop, hid):
                tile = slice(top, top + hid)
                g = grad[tile, at] * (0.5 + slope[tile, at].astype(F32))
                grad_b[tile, at] = g.astype(BF16)
                total = total + (g[:, :LANES] + g[:, LANES:])
        writes[n].start()
    for copy in late[1]:
        copy.wait()
    results.append(products(1))
    spectra = jnp.concatenate([r[0] for r in results], axis=1)
    each = hid // owners
    pack_spectra(spectra, rows_out, 8 + 2 * each, layers, cells, owners, owned)
    part_in, part_out = results[0][1] + results[1][1], results[0][2] + results[1][2]
    bias = jnp.sum(total, axis=1, keepdims=True)
    zeros = jnp.zeros((hid, LANES - 2 * chans), F32)
    full = jnp.concatenate([part_in, part_out, zeros], axis=1)
    full = jnp.where(iota((hid, LANES), 1) == 2 * chans, bias, full)
    high = full.astype(BF16).astype(F32)
    for at, value in enumerate((high, full - high)):
        slab[...] = value
        for row in range(each):
            rows_out[pl.ds(8 + at * each + row, owners, 8 + 2 * each), :] = slab[pl.ds(row, owners, each), :]
    out[...] = rows_out[...].reshape(out.shape).astype(BF16)
    writes.append(load(out, out_h, outs.at[2]))
    writes[2].start()
    for write in writes:
        write.wait()


def mlp_grad_kernel(cot_h, grad_h, w_in_h, *refs, count, carried):
    sources, out, targets, refs = refs[:carried], refs[carried], refs[carried + 1 : 2 * carried + 1], refs[2 * carried + 1 :]
    cot, grad_b, w_in, sems = refs
    chans, hid = w_in.shape
    half = cot.shape[0] // 2
    copies = [load(w_in_h, w_in, sems.at[0])]
    for n in range(2):
        low, high = pl.ds(n * half, half), pl.ds(n * half // chans * hid, half // chans * hid)
        copies.append(load(cot_h.at[low, :], cot.at[low, :], sems.at[1 + 2 * n]))
        copies.append(load(grad_h.at[high, :], grad_b.at[high, :], sems.at[2 + 2 * n]))
    copies += [load(a, b, sems.at[5 + n]) for n, (a, b) in enumerate(zip(sources, targets))]
    for copy in copies:
        copy.start()
    copies[0].wait()
    weights = by_cell(w_in[...].astype(F32), count)
    for n in range(2):
        for copy in copies[1 + 2 * n : 3 + 2 * n]:
            copy.wait()
        low = slice(n * half, (n + 1) * half)
        high = slice(low.start // chans * hid, low.stop // chans * hid)
        for left in range(0, cot.shape[1], STEP):
            at = slice(left, left + STEP)
            out[low, at] = cot[low, at].astype(F32) + dot(weights, grad_b[high, at])
    for copy in copies[5:]:
        copy.wait()


def back_kernel(
    blocks, weights, forward, inverse, _, out_h, modes_h, out, modes, rows_ref, sems, *, sizes, each,
):
    layers, cells, owners, owned = sizes
    chans = LANES // (layers * owned)
    spread = spread_table(chans, layers * owned)
    collect = collect_table(chans)
    spectra = unpack(blocks, rows_ref, cells, owners)
    z = modes_of(spectra, forward)
    modes[...] = z
    save = load(modes, modes_h, sems.at[0])
    save.start()
    totals = []
    for row in range(each):
        at = 8 + row
        total = jnp.sum(
            rows_ref[pl.ds(at, owners, 8 + 2 * each), :] + rows_ref[pl.ds(at + each, owners, 8 + 2 * each), :],
            axis=0,
            keepdims=True,
        )
        totals.append(total)
    half = z.shape[0] // 2
    high, low = split(z)
    wide = dot(jnp.concatenate([high, low], axis=1), spread)
    pieces = []
    for mode in range(owned):
        acc = None
        for left in range(0, weights.shape[3], CHUNK):
            wr = weights[0, mode, :, left : left + CHUNK].astype(F32)
            wi = weights[1, mode, :, left : left + CHUNK].astype(F32)
            terms = []
            for layer in range(layers):
                pick = (mode * layers + layer) * LANES
                g = jnp.concatenate([wide[:, pick : pick + LANES]] * (CHUNK // LANES), axis=1)
                gr, gi = g[:half], g[half:]
                terms += [(gr * wr + gi * wi).astype(BF16), (gi * wr - gr * wi).astype(BF16)]
            s = dot(jnp.concatenate(terms, axis=0), collect[left : left + CHUNK, :])
            acc = s if acc is None else acc + s
        acc = [acc[2 * n * half : 2 * (n + 1) * half] for n in range(layers)]
        pieces += [a[:, :chans] for a in acc]
    fields_of(jnp.concatenate(pieces, axis=1), inverse, rows_ref, 8 + 2 * each, cells, owners)
    for row, total in enumerate(totals):
        high = total.astype(BF16).astype(F32)
        rows_ref[pl.ds(8 + row, owners, 8 + 2 * each), :] = jnp.broadcast_to(high, (owners, LANES))
        rows_ref[pl.ds(8 + each + row, owners, 8 + 2 * each), :] = jnp.broadcast_to(total - high, (owners, LANES))
    out[...] = rows_ref[...].reshape(out.shape).astype(BF16)
    send = load(out, out_h, sems.at[1])
    send.start()
    save.wait()
    send.wait()


def weight_grad_kernel(zx_h, zg_h, out_h, zx, zg, out, sems, *, sizes, factor):
    layers, owned = sizes[0], sizes[3]
    chans = LANES // (layers * owned)
    copies = [load(a, b, sems.at[n]) for n, (a, b) in enumerate(((zx_h, zx), (zg_h, zg)))]
    for copy in copies:
        copy.start()
    expand = expand_table(chans, chans * chans)
    spread = spread_table(chans, layers * owned)
    for copy in copies:
        copy.wait()
    z = zx[...] * factor
    half = z.shape[0] // 2
    high, low = split(zg[...])
    wide = dot(jnp.concatenate([high, low], axis=1), spread)
    saves = []
    for mode in range(owned):
        split_z = [widen(z, mode * layers + layer, chans) for layer in range(layers)]
        for left in range(0, out.shape[3], CHUNK):
            real = imag = 0.0
            for layer in range(layers):
                x = dot(split_z[layer], expand[:, left : left + CHUNK])
                xr, xi = x[:half], x[half:]
                pick = (mode * layers + layer) * LANES
                g = jnp.concatenate([wide[:, pick : pick + LANES]] * (CHUNK // LANES), axis=1)
                gr, gi = g[:half], g[half:]
                real = real + (xr * gr + xi * gi)
                imag = imag + (xr * gi - xi * gr)
            out[0, mode, :, left : left + CHUNK] = real
            out[1, mode, :, left : left + CHUNK] = imag
        for part in range(2):
            saves.append(
                load(out.at[part, mode], out_h.at[part, mode], sems.at[2 + part * owned + mode])
            )
            saves[-1].start()
    for save in saves:
        save.wait()


def final_kernel(
    blocks, base, inv, _, out_h, in_h, out_w_h, bias_h, out, rows_ref, slab, turned, outs, *, sizes, norm,
):
    layers, cells, owners, owned = sizes
    chans = in_h.shape[0]
    count = 4
    span = base.shape[0] // count
    waves = phi_rows(blocks, rows_ref, layers, cells, owners, owned)
    hid = slab.shape[0]
    each = hid // owners
    for row in range(each):
        slab[pl.ds(row, owners, each), :] = (
            rows_ref[pl.ds(8 + row, owners, 8 + 2 * each), :] + rows_ref[pl.ds(8 + each + row, owners, 8 + 2 * each), :]
        ) * norm
    turned[...] = slab[...].T
    writes = [
        load(turned.at[pl.ds(n * chans, h.shape[0]), :], h, outs.at[1, n])
        for n, h in enumerate((in_h, out_w_h, bias_h))
    ]
    for write in writes:
        write.start()
    for j in range(count):
        here, rows = slice(j * span, (j + 1) * span), pl.ds(j * span, span)
        for left in range(0, base.shape[1], STEP):
            at = slice(left, left + STEP)
            out[here, at] = base[here, at] + dot(waves[here], inv[:, at])
        writes.append(load(out.at[rows, :], out_h.at[rows, :], outs.at[0, j]))
        writes[-1].start()
    for write in writes:
        write.wait()


def call(kernel, ins, outs, scratch, flops, *args, **static):
    space = {"h": pltpu.HBM, "v": pltpu.VMEM, "w": pltpu.VMEM}
    keep = {"h": pltpu.HBM, "w": pltpu.VMEM}
    shapes = [jax.ShapeDtypeStruct(s, d) for _, s, d in outs]
    size = lambda x: math.prod(x.shape) * x.dtype.itemsize
    moved = sum(size(x) for x in (*args, *shapes))
    args = [
        pltpu.with_memory_space_constraint(x, keep[k]) if k in keep else x
        for k, x in zip(ins, args)
    ]
    return pl.pallas_call(
        functools.partial(kernel, **static),
        out_shape=[
            keep[o[0]](x.shape, x.dtype) if o[0] in keep else x for o, x in zip(outs, shapes)
        ],
        in_specs=[pl.BlockSpec(memory_space=space[k]) for k in ins],
        out_specs=[pl.BlockSpec(memory_space=space[k]) for k, _, _ in outs],
        scratch_shapes=[
            pltpu.SemaphoreType.DMA(s) if d is None else pltpu.VMEM(s, d) for s, d in scratch
        ],
        compiler_params=pltpu.CompilerParams(vmem_limit_bytes=LIMIT),
        cost_estimate=pl.CostEstimate(
            flops=flops,
            bytes_accessed=moved,
            transcendentals=0,
        ),
    )(*args)


def local(field_in, grad_out, spectral_weight, mlp_in, mlp_bias, mlp_out):
    layers, cells, chans, n_phi = field_in.shape
    owners = lax.axis_size("eta")
    depth = lax.axis_size("depth")
    n_eta = cells * owners
    owned = spectral_weight.shape[1]
    n_eta_modes = spectral_weight.shape[2]
    n_phi_modes = owned * owners
    hid = mlp_in.shape[1]
    count = layers * cells
    each = hid // owners
    sizes = (layers, cells, owners, owned)
    pairs = phi_pairs(n_phi, owned, owners)
    phi_fwd = jnp.asarray(pairs / math.sqrt(n_phi), BF16)
    phi_inv = jnp.asarray(pairs / math.sqrt(n_phi_modes), BF16)
    forward, inverse = eta_tables(cells, owners, n_eta_modes)
    forward = jnp.asarray(forward, BF16)
    inverse_high = inverse.astype(BF16)
    inverse_low = (inverse - inverse_high.astype(np.float64)).astype(BF16)
    inverse = jnp.asarray(np.concatenate([inverse_high, inverse_high, inverse_low], axis=1))

    thin = (count * chans, n_phi)
    tall = (count * hid, n_phi)
    field = field_in.reshape(thin)
    cot = grad_out.reshape(thin)
    w_out = mlp_out.T
    steps = n_phi // STEP
    exchange = lambda x: lax.all_to_all(x, "eta", 0, 0, tiled=True)
    exchange_pairs = lambda x: exchange(x.reshape(owners, -1, 2, LANES)).reshape(x.shape)
    small = (owners, 8, LANES)
    large = (owners * (8 + 2 * each), LANES)
    modes = (2 * n_eta_modes, LANES)
    small_rows = ((owners * 8, LANES), F32)
    large_rows = (large, F32)
    table = ((2 * n_phi_modes, n_phi), BF16)
    grid_mul = 2 * count * n_phi * chans

    smalls = (mlp_in, mlp_bias[None], w_out)
    mixing = (spectral_weight, forward, inverse)
    half = count // 2
    half_thin = (half * chans, n_phi)
    xp, field_a, field_b, w_in_v, bias_v, w_out_v = call(
        xp_kernel, "hhhhh",
        [("h", small, BF16), *[("w", half_thin, BF16)] * 2, *(("w", x.shape, x.dtype) for x in smalls)],
        [(small, BF16), table, small_rows, ((7,), None)],
        grid_mul * 2 * n_phi_modes, phi_fwd, field, *smalls, sizes=sizes,
    )
    xp = exchange(xp)
    part = (half * hid, n_phi)

    def hidden_half(field, after, keep_base, *carried):
        return call(
            hidden_kernel, "wwwwh" + "h" * len(carried),
            [
                ("h", part, BF16), ("h", part, BF16), (keep_base, half_thin, F32),
                *(("w", x.shape, x.dtype) for x in carried),
            ],
            [
                ((hid, CHUNK), F32), (part, F32), (part, BF16), (part, BF16),
                ((len(carried),), None), ((3, steps), None),
                *([(half_thin, F32)] if keep_base == "h" else []),
            ],
            grid_mul * hid, field, w_in_v, bias_v, w_out_v, after, *carried,
            count=half, carried=len(carried),
        )

    hidden_a, slope_a, base_a, weights, forward, inverse = hidden_half(
        field_a, w_out, "w", *mixing
    )
    wx, zx = call(
        mix_kernel, "vwww", [("h", small, BF16), ("h", modes, F32)],
        [(small, BF16), (modes, F32), small_rows, ((2,), None)],
        1 << 24, xp, weights, forward, inverse, sizes=sizes,
    )
    wx = exchange(wx)
    hidden_b, slope_b, base_b, cot_v, inv_v = hidden_half(field_b, zx, "h", cot, phi_inv)
    gp, hidden_gb = call(
        gpre_kernel, "vwwwwhhhhhhh", [("h", large, BF16), ("h", tall, BF16)],
        [
            (large, BF16), (thin, BF16), (tall, BF16), (tall, BF16), (half_thin, F32), table,
            (thin, BF16), (tall, BF16),
            ((count * chans, 2 * n_phi_modes), BF16), ((half * hid, half * chans), BF16),
            (thin, F32), (tall, F32), small_rows, large_rows, ((hid, LANES), F32),
            ((3, 3), None), ((3,), None),
        ],
        grid_mul * (4 * n_phi_modes + 4 * hid), wx, cot_v, base_a, inv_v, w_out_v,
        field, hidden_a, hidden_b, slope_a, slope_b, base_b, phi_fwd, sizes=sizes,
    )
    gp = exchange_pairs(gp)
    carried = (phi_inv, *mixing)
    partial, inverse_phi, weights, forward, inverse = call(
        mlp_grad_kernel, "hhh" + "h" * len(carried),
        [("w", thin, F32), *(("w", x.shape, x.dtype) for x in carried)],
        [(thin, BF16), (tall, BF16), (mlp_in.shape, BF16), ((5 + len(carried),), None)],
        grid_mul * hid, cot, hidden_gb, mlp_in, *carried, count=half, carried=len(carried),
    )
    wb, zg = call(
        back_kernel, "vwwww", [("h", large, BF16), ("h", modes, F32)],
        [(large, BF16), (modes, F32), large_rows, ((2,), None)],
        1 << 24, gp, weights, forward, inverse, partial, sizes=sizes, each=each,
    )
    wb = exchange_pairs(wb)
    factor = math.sqrt(n_phi * n_eta / (n_phi_modes * n_eta_modes))
    grad_shape = (2, owned, n_eta_modes, chans * chans)
    (grad_spectral,) = call(
        weight_grad_kernel, "hh", [("h", grad_shape, F32)],
        [(modes, F32), (modes, F32), (grad_shape, F32), ((2 + 2 * owned,), None)],
        1 << 24, zx, zg, sizes=sizes, factor=factor,
    )
    norm = 1.0 / math.sqrt(layers * depth * n_eta * n_phi)
    grad_in, total_in, total_out, total_bias = call(
        final_kernel, "vwwh",
        [("h", thin, F32), ("h", (chans, hid), F32), ("h", (chans, hid), F32), ("h", (1, hid), F32)],
        [
            (thin, F32), large_rows, ((hid, LANES), F32), ((LANES, hid), F32), ((2, 4), None),
        ],
        grid_mul * 2 * n_phi_modes, wb, partial, inverse_phi, grad_spectral, sizes=sizes, norm=norm,
    )
    if depth > 1:
        grad_spectral = lax.psum_scatter(grad_spectral, "depth", scatter_dimension=2, tiled=True)
        total_in, total_out, total_bias = lax.psum((total_in, total_out, total_bias), "depth")
    return (grad_in.reshape(field_in.shape), grad_spectral, total_in, total_out.T, total_bias[0])


def solution(mesh):
    return jax.shard_map(
        local,
        mesh=mesh,
        in_specs=(
            P("depth", "eta", None, None),
            P("depth", "eta", None, None),
            P(None, "eta", None, None),
            P(),
            P(),
            P(),
        ),
        out_specs=(P("depth", "eta", None, None), P(None, "eta", "depth", None), P(), P(), P()),
        check_vma=False,
    )
```
